32 devices in a mesh: groups: 2 (over x), tiles: 16 (over z, y, core).
Axes of the slice: x: 2, y: 2, z: 4, core: 2. Of those that a mesh axis runs over, the one named last changes fastest.
Arguments:
- tiles: bfloat16 [3, 8192], P(None, ('groups', 'tiles')), parts along dimension 1, may hold values from 0 to 1
- tile_slide: int32 [128], P(('groups', 'tiles')), parts along dimension 0, may hold values from 0 to 383
- tile_mask: int32 [128], P(('groups', 'tiles')), parts along dimension 0, may hold values from 0 to 1, as said below
- tile_label: int32 [128], P(('groups', 'tiles')), parts along dimension 0, may hold values from 0 to 8
- attack_field: float32 [49152], P(('groups', 'tiles')), parts along dimension 0, may hold values from -1 to 1
- lift_weight: float32 [9, 3, 128], replicated, may hold values from -1.25 to 1.25
- group_weight: bfloat16 [8, 9, 128, 128], replicated, may hold values from -0.0625 to 0.0625
- class_weight: float32 [128, 9], replicated, may hold values from -0.5 to 0.5
Outputs:
- margins: float32 [128], P(('groups', 'tiles')), parts along dimension 0
- attack_grad: float32 [49152], P(('groups', 'tiles')), parts along dimension 0
The draws below stay inside these ranges and needn't reach their ends.
There are 2 independent parts, one for each index of `groups`. The reference program is written for one: setup_inputs(seed, part) draws one part's arguments, and reference() takes and returns one part's arrays. A program takes and returns all parts, laid end to end along the dimension named above; an argument that names none is the same for every part. Nothing has to cross between parts.
Inputs may be any that keep to these rules, and one draw needn't show every extreme that they name: `tile_mask`: in every part the live tiles number exactly 2 times the devices of the tiles axis in all; one device holds 0 to 4 of them, and on some device all 4 slots are live.
All inputs are finite; a program needn't handle non-finite values.
Results may differ from the reference program's by a relative error of at most 0.007.
Values may be sent and summed in bfloat16 or wider, within the bound.
No kernel may reach another device: no remote copies, remote signals or barrier semaphores. Data moves between devices by JAX's collectives and lax.ppermute only.
A program may use at most 128 MiB of HBM per device.

```python
import math
import jax
import jax.numpy as jnp
import numpy as np
from jax import lax

HUES = 8
CH = 128
CLASSES = 9
TILE = 8
PIX = 64
BAL = 2
CAP = 4
SLIDES = 384
TOTAL_SLOTS = 64
N_TILES = 16


def draw_tile_mask(key, part):
    base_key = jax.random.fold_in(key, 101)
    key_list = jax.random.split(base_key, 4)
    device_order = jax.random.permutation(key_list[0], N_TILES)
    shift_amount = jax.random.randint(key_list[1], (N_TILES // 2,), -BAL, BAL + 1)
    chosen_pair = jax.random.randint(key_list[2], (), 0, N_TILES // 2)
    shift_amount = jnp.where(jnp.arange(N_TILES // 2) == chosen_pair, BAL, shift_amount)
    pair_loads = jnp.stack([BAL + shift_amount, BAL - shift_amount], axis=1).reshape(N_TILES)
    tile_loads = jnp.zeros((N_TILES,), jnp.int32).at[device_order].set(pair_loads.astype(jnp.int32))
    priority = jax.vmap(lambda device_key: jax.random.permutation(device_key, CAP))(jax.random.split(key_list[3], N_TILES))
    live_mask = (priority < tile_loads[:, None]).astype(jnp.int32)
    return live_mask.reshape(N_TILES * CAP)


def set_ends(values, stream_key, least, largest):
    dims = values.shape
    spot = [jax.random.randint(jax.random.fold_in(stream_key, axis), (), 0, dims[axis]) for axis in range(len(dims))]
    values = values.at[tuple(spot)].set(least)
    longest = dims.index(max(dims))
    spot[longest] = (spot[longest] + 1) % dims[longest]
    return values.at[tuple(spot)].set(largest)


def shard_levels(own_key, dims, cuts, low, top_value):
    gain = 1.0
    for position, parts in cuts:
        heights = jax.random.uniform(jax.random.fold_in(jax.random.fold_in(own_key, 6), position), (parts,), jnp.float32, low / len(cuts), top_value / len(cuts))
        gain = gain * jnp.repeat(jnp.exp(heights), dims[position] // parts).reshape((-1,) + (1,) * (len(dims) - 1 - position))
    return gain


def gaussian(key, extent, spread, reach, kind=jnp.bfloat16):
    values = jax.random.normal(key, extent, jnp.float32) * spread
    return jnp.minimum(jnp.maximum(values, -reach), reach).astype(kind)


def setup_inputs(seed: int = 0, part: int = 0) -> dict:
    keys = jax.random.split(jax.random.key(seed), 9)
    part_splits = jax.random.split(jax.random.fold_in(keys[8], part), 9)
    return {
        "tiles": jnp.clip(1.0 * jax.random.uniform(part_splits[0], (3, TOTAL_SLOTS * PIX), jnp.float32) ** shard_levels(part_splits[0], (3, TOTAL_SLOTS * PIX), ((1, 16),), -0.2, 0.2), 0.0, 1.0).astype(jnp.bfloat16),
        "tile_slide": set_ends(jax.random.randint(part_splits[1], (TOTAL_SLOTS,), 0, SLIDES), jax.random.fold_in(part_splits[1], 1), 0, SLIDES - 1).astype(jnp.int32),
        "tile_mask": draw_tile_mask(jax.random.fold_in(jax.random.fold_in(keys[8], part), 71), part),
        "tile_label": set_ends(jax.random.randint(part_splits[3], (TOTAL_SLOTS,), 0, CLASSES), jax.random.fold_in(part_splits[3], 1), 0, CLASSES - 1).astype(jnp.int32),
        "attack_field": jnp.clip(jax.random.uniform(part_splits[4], (SLIDES * PIX,), jnp.float32, -1.0, 1.0) * shard_levels(part_splits[4], (SLIDES * PIX,), ((0, 16),), -0.4, 0.0), -1.0, 1.0),
        "lift_weight": gaussian(keys[5], (9, 3, CH), 27 ** -0.5, 1.25, jnp.float32),
        "group_weight": gaussian(keys[6], (HUES, 9, CH, CH), (9 * HUES * CH) ** -0.5, 0.0625),
        "class_weight": gaussian(keys[7], (CH, CLASSES), CH ** -0.5, 0.5, jnp.float32),
    }


def hue_rotations(hue_count):
    factor = 1.0 / math.sqrt(3.0)
    skew_part = factor * np.array([[0.0, -1.0, 1.0], [1.0, 0.0, -1.0], [-1.0, 1.0, 0.0]])
    result = []
    for number in range(hue_count):
        rotation_angle = -2.0 * math.pi * number / hue_count
        result.append(math.cos(rotation_angle) * np.eye(3) + math.sin(rotation_angle) * skew_part + (1.0 - math.cos(rotation_angle)) * np.ones((3, 3)) / 3.0)
    return np.stack(result)

def lift_matrix(lift_weight, hue_count):
    rotations = jnp.asarray(hue_rotations(hue_count), dtype=jnp.float32)
    mapped = jnp.einsum('tio,kij->tjko', lift_weight.astype(jnp.float32), rotations, precision=lax.Precision.HIGHEST)
    return mapped.reshape(27, hue_count * lift_weight.shape[2])

def circulant(group_weight, tap_index):
    hue_count = group_weight.shape[0]
    channels = group_weight.shape[2]
    index_table = np.array([[(source - target) % hue_count for target in range(hue_count)] for source in range(hue_count)], dtype=np.int32)
    blocks = group_weight[:, tap_index][index_table]
    return blocks.transpose(0, 2, 1, 3).reshape(hue_count * channels, hue_count * channels)

def grey_cross(colours):
    factor = 1.0 / math.sqrt(3.0)
    red_part = colours[:, 0]
    green_part = colours[:, 1]
    blue_part = colours[:, 2]
    return factor * jnp.stack([blue_part - green_part, red_part - blue_part, green_part - red_part], axis=1)

def neighbours(feature, tap_index, forward):
    tile_side = feature.shape[1]
    padded = jnp.pad(feature, ((0, 0), (1, 1), (1, 1), (0, 0)))
    row_start = tap_index // 3
    column_start = tap_index % 3
    if not forward:
        row_start = 2 - row_start
        column_start = 2 - column_start
    return padded[:, row_start:row_start + tile_side, column_start:column_start + tile_side]

def silu_slope(values):
    logistic = jax.nn.sigmoid(values)
    return logistic * (1.0 + values * (1.0 - logistic))

def tile_attack(pixels, angles, score_grad, lifting, circulants, class_weight):
    slot_count = pixels.shape[0]
    channels = class_weight.shape[0]
    width = circulants.shape[1]
    hue_count = width // channels
    tile_side = TILE
    pixel_count = tile_side * tile_side
    colours = pixels.astype(jnp.float32)
    cos_angle = jnp.cos(angles)[:, None, :]
    sin_angle = jnp.sin(angles)[:, None, :]
    cross_term = grey_cross(colours)
    grey_level = lax.optimization_barrier(jnp.mean(colours, axis=1, keepdims=True))
    attacked = cos_angle * colours + sin_angle * cross_term + (1.0 - cos_angle) * grey_level
    picture = attacked.reshape(slot_count, 3, tile_side, tile_side).transpose(0, 2, 3, 1)
    patches = jnp.concatenate([neighbours(picture, tap_index, True) for tap_index in range(9)], axis=3)
    patches = patches.reshape(slot_count * pixel_count, 27)
    lifted = jnp.dot(patches, lifting, precision=lax.Precision.HIGHEST, preferred_element_type=jnp.float32)
    activated = jax.nn.silu(lifted).astype(jnp.bfloat16).reshape(slot_count, tile_side, tile_side, width)
    mixed = jnp.zeros((slot_count * pixel_count, width), jnp.float32)
    for tap_index in range(9):
        shifted = neighbours(activated, tap_index, True).reshape(slot_count * pixel_count, width)
        mixed = mixed + jnp.dot(shifted, circulants[tap_index], preferred_element_type=jnp.float32)
    pooled = lax.optimization_barrier(jnp.mean(jax.nn.silu(mixed).reshape(slot_count, pixel_count * hue_count, channels), axis=1))
    scores = jnp.dot(pooled, class_weight, precision=lax.Precision.HIGHEST, preferred_element_type=jnp.float32)
    margins = -lax.optimization_barrier(jnp.sum(score_grad * scores, axis=1)) / pixel_count
    pooled_grad = lax.dot_general(score_grad, class_weight, (((1,), (1,)), ((), ())), precision=lax.Precision.HIGHEST, preferred_element_type=jnp.float32)
    spread_grad = jnp.broadcast_to((pooled_grad / (hue_count * pixel_count))[:, None, :], (slot_count, pixel_count * hue_count, channels))
    spread_grad = spread_grad.reshape(slot_count * pixel_count, width)
    mixed_grad = (spread_grad * silu_slope(mixed)).astype(jnp.bfloat16)
    mixed_grad = mixed_grad.reshape(slot_count, tile_side, tile_side, width)
    act_grad = jnp.zeros((slot_count * pixel_count, width), jnp.float32)
    for tap_index in range(9):
        shifted = neighbours(mixed_grad, tap_index, False).reshape(slot_count * pixel_count, width)
        act_grad = act_grad + lax.dot_general(shifted, circulants[tap_index], (((1,), (1,)), ((), ())), preferred_element_type=jnp.float32)
    lifted_grad = act_grad * silu_slope(lifted)
    patch_grad = lax.dot_general(lifted_grad, lifting, (((1,), (1,)), ((), ())), precision=lax.Precision.HIGHEST, preferred_element_type=jnp.float32)
    patch_grad = patch_grad.reshape(slot_count, tile_side, tile_side, 9, 3)
    picture_grad = jnp.zeros((slot_count, tile_side, tile_side, 3), jnp.float32)
    for tap_index in range(9):
        picture_grad = picture_grad + neighbours(patch_grad[:, :, :, tap_index, :], tap_index, False)
    colour_grad = picture_grad.transpose(0, 3, 1, 2).reshape(slot_count, 3, pixel_count)
    turning = -sin_angle * colours + cos_angle * cross_term + sin_angle * grey_level
    angle_grad = lax.optimization_barrier(jnp.sum(colour_grad * turning, axis=1))
    return (angle_grad, margins)

def reference(tiles, tile_slide, tile_mask, tile_label, attack_field, lift_weight, group_weight, class_weight):
    live_total = N_TILES * BAL
    picked = jnp.nonzero(tile_mask, size=live_total)[0].astype(jnp.int32)
    pixels = tiles.reshape(3, TOTAL_SLOTS, PIX).transpose(1, 0, 2)[picked]
    slides = tile_slide[picked]
    classes = class_weight.shape[1]
    label_hot = (tile_label[picked][:, None] == jnp.arange(classes, dtype=jnp.int32)[None, :]).astype(jnp.float32)
    score_grad = PIX * (1.0 / classes - label_hot)
    angles = attack_field.reshape(SLIDES, PIX)[slides]
    lifting = lift_matrix(lift_weight, group_weight.shape[0])
    circulants = jnp.stack([circulant(group_weight, tap_index) for tap_index in range(9)])
    block_total = N_TILES // 8

    def attack_block(inputs):
        return tile_attack(inputs[0], inputs[1], inputs[2], lifting, circulants, class_weight)
    angle_grad, margins_live = lax.map(attack_block, (pixels.reshape(block_total, 8 * BAL, 3, PIX), angles.reshape(block_total, 8 * BAL, PIX), score_grad.reshape(block_total, 8 * BAL, classes)))
    angle_grad = angle_grad.reshape(live_total, PIX)
    margins_live = margins_live.reshape(live_total)
    raw_sums = jax.ops.segment_sum(angle_grad, slides, num_segments=SLIDES)
    counts = jax.ops.segment_sum(jnp.ones((live_total,), jnp.float32), slides, num_segments=SLIDES)
    attack_grad = (raw_sums / jnp.maximum(counts, 1.0)[:, None]).reshape(SLIDES * PIX)
    margins = jnp.zeros((TOTAL_SLOTS,), jnp.float32).at[picked].set(margins_live)
    return (margins, attack_grad)
```

```python
import functools
import math

import jax
import jax.numpy as jnp
from jax import lax
from jax.experimental import pallas as pl
from jax.experimental.pallas import tpu as pltpu
from jax.sharding import PartitionSpec as P

F32 = jnp.float32
BF16 = jnp.bfloat16
PIX = 64
ROWS = 32
INFO = 64
GROUP = 16
CHUNK = 4
SKEW = 1.0 / math.sqrt(3.0)
HALF = math.sqrt(0.5)


def iota(shape, axis):
    return lax.broadcasted_iota(jnp.int32, shape, axis)


def dot(a, b, dims, precision=None):
    return lax.dot_general(a, b, (dims, ((), ())), precision=precision, preferred_element_type=F32)


NN = ((1,), (0,))
NT = ((1,), (1,))
TN = ((0,), (0,))


def hue_fourier(x):
    s = [x[i] + x[i + 4] for i in range(4)]
    d = [x[i] - x[i + 4] for i in range(4)]
    e, o = s[0] + s[2], s[1] + s[3]
    dm, dp = (d[1] - d[3]) * HALF, (d[1] + d[3]) * HALF
    return [e + o, e - o, d[0] + dm, -d[2] - dp, s[0] - s[2], s[3] - s[1], d[0] - dm, d[2] - dp]


def hue_inverse(c):
    f0, f4, r1, i1, r2, i2, r3, i3 = c
    a, b = f0 + f4, f0 - f4
    s0, s2, s1, s3 = a + r2, a - r2, b - i2, b + i2
    d0, d2 = r1 + r3, i3 - i1
    p, q = (r1 - r3) * HALF, (i1 + i3) * HALF
    d1, d3 = p - q, -p - q
    s, d = (s0, s1, s2, s3), (d0, d1, d2, d3)
    return [s[k] + d[k] for k in range(4)] + [s[k] - d[k] for k in range(4)]


def pack_kernel(slides, slide_ref, mask_ref, label_ref, tiles_ref, field_ref, out_ref):
    lane = iota((1, 128), 1)
    left = lane < PIX
    tiles = tiles_ref[...].astype(F32)
    rows, parts = [], []
    for slot in range(4):
        part = tiles[:, 128 * (slot // 2) : 128 * (slot // 2) + 128]
        turned = pltpu.roll(part, PIX, 1)
        low, high = (part, turned) if slot % 2 == 0 else (turned, part)
        slide = slide_ref[slot]
        owner = slide // slides
        place = slide - owner * slides
        facts = [owner, place // 2, mask_ref[slot], label_ref[slot], slot, place % 2]
        info = jnp.zeros((1, 128), jnp.int32)
        for number, fact in enumerate(facts):
            info = jnp.where(lane == INFO + number, fact, info)
        rows.append(jnp.where(left, low[0:1], high[1:2]))
        rows.append(jnp.where(left, low[2:3], info.astype(F32)))
    rows = jnp.concatenate(rows, axis=0)
    field = field_ref[...]
    upper = field.astype(BF16).astype(F32)
    rest = jnp.concatenate([upper, field - upper], axis=0)
    at = (iota((8, 128), 1) == INFO + 6) & (iota((8, 128), 0) % 2 == 1)
    for target in range(out_ref.shape[0]):
        slot_rows = jnp.where(at, float(target), rows)
        out_ref[target] = jnp.concatenate([slot_rows, rest], axis=0).astype(BF16)


def weight_kernel(weight_ref, lift_ref, out_ref, forward_ref, backward_ref):
    for block in range(0, 128, 32):
        rows = slice(block, block + 32)
        f0, f4, r1, i1, r2, i2, r3, i3 = hue_fourier([weight_ref[k, 0, rows, :].astype(F32) for k in range(8)])
        zero = jnp.zeros((32, 128), F32)
        parts = [(f0 * 0.0625, zero, zero, f4 * 0.0625)]
        for re, im in ((r1, i1), (r2, i2), (r3, i3)):
            re, im = re * 0.125, im * 0.125
            parts.append((re, -im, im, re))
        for f, (a, b, c, d) in enumerate(parts):
            out_ref[f, 0, rows, 0:128] = a.astype(BF16)
            out_ref[f, 0, rows, 128:256] = b.astype(BF16)
            out_ref[f, 0, block + 128 : block + 160, 0:128] = c.astype(BF16)
            out_ref[f, 0, block + 128 : block + 160, 128:256] = d.astype(BF16)

    @pl.when(pl.program_id(0) == 0)
    def _():
        both, single = [], []
        for tap in range(9):
            lift = lift_ref[tap]
            l0, l1, l2 = lift[0:1], lift[1:2], lift[2:3]
            grey = (l0 + l1 + l2) * (1.0 / 3.0)
            zero = jnp.zeros((1, 128), F32)
            columns = (
                [grey] * 3,
                [l0 - grey, l1 - grey, l2 - grey],
                [(l1 - l2) * SKEW, (l2 - l0) * SKEW, (l0 - l1) * SKEW],
            )
            both.append(jnp.concatenate([jnp.concatenate([*c, zero, *c, zero], axis=0) for c in columns], axis=1))
            single.append(jnp.concatenate([jnp.concatenate([*c, *[zero] * 5], axis=0) for c in columns], axis=1))
        both = jnp.concatenate(both, axis=0) * 0.5
        upper = both.astype(BF16).astype(F32)
        forward_ref[...] = jnp.concatenate([upper, both - upper], axis=0).astype(BF16)
        single = jnp.concatenate(single + [jnp.zeros((8, 384), F32)], axis=0)
        upper = single.astype(BF16).astype(F32)
        backward_ref[...] = jnp.concatenate([upper, upper, single - upper], axis=1).astype(BF16)


def tap_mask(dy, dx):
    lane = iota((1, 128), 1)
    x, y = lane % 8 + dx, (lane // 8) % 8 + dy
    return (x >= 0) & (x < 8) & (y >= 0) & (y < 8)


def shifted(value, by):
    return value if by % 128 == 0 else pltpu.roll(value, (-by) % 128, 1)


def main_kernel(
    got_ref, weight_hbm, forward_ref, backward_ref, class_ref,
    margin_ref, grad_ref,
    weight_ref, key_ref, att_ref, turn_ref, pg_ref, place_ref, slot_ref,
    lift_ref, slope_ref, act_ref, mix_ref, pool_ref, back_ref, sum_ref, count_ref, weight_sem,
):
    total = got_ref.shape[0] * ROWS
    copy = pltpu.make_async_copy(weight_hbm, weight_ref, weight_sem)
    copy.start()
    got = got_ref[...].reshape(total, 128)

    picker = (iota((8, 128), 1) == INFO + iota((8, 128), 0)).astype(BF16)
    facts = dot(picker, got, NT)
    spot = iota((1, total), 1)
    within = spot % ROWS
    is_slot = (within < 8) & (within % 2 == 1)
    live = is_slot & (facts[2:3] > 0.5)
    me = facts[6:7]
    mine = live & (facts[0:1] == me)
    here = live & ((spot // ROWS).astype(F32) == me)
    marks = jnp.concatenate([mine.astype(F32), here.astype(F32), jnp.zeros((6, total), F32)], axis=0)
    before = (iota((128, 128), 0) < iota((128, 128), 1)).astype(BF16)
    carry, ranks = jnp.zeros((8, 1), F32), []
    for block in range(total // 128):
        part = marks[:, block * 128 : block * 128 + 128]
        ranks.append(dot(part.astype(BF16), before, NN) + carry)
        carry = carry + jnp.sum(part, axis=1, keepdims=True)
    ranks = jnp.concatenate(ranks, axis=1)
    owned = carry[0:1]
    key_mine = jnp.where(mine, ranks[0:1], -1.0)
    key_here = jnp.where(here, ranks[1:2] + owned, -1.0)
    key_ref[...] = jnp.concatenate([key_mine, key_here, jnp.full((6, total), -1.0, F32)], axis=0)
    owned_count = jnp.sum(carry[0:1]).astype(jnp.int32)
    item_count = owned_count + jnp.sum(carry[1:2]).astype(jnp.int32)

    sum_ref[...] = jnp.zeros_like(sum_ref)
    count_ref[...] = jnp.zeros_like(count_ref)
    margin_ref[...] = jnp.zeros_like(margin_ref)
    act_ref[:, 0:32, :] = jnp.zeros((3, 32, 1024), BF16)
    act_ref[:, 288:320, :] = jnp.zeros((3, 32, 1024), BF16)

    height = GROUP * 4
    row8 = iota((height, 128), 0) % 8
    lane = iota((height, 128), 1)
    odd = row8 >= 4
    colour = row8 % 4
    lane_half = lane >= PIX

    def gather(group):
        item = (group * GROUP + 2 * (iota((height, 1), 0) // 8) + (iota((height, 1), 0) % 8) // 4).astype(F32)
        keys = key_ref[...]
        earlier = pltpu.roll(keys, total - 1, 1)
        second = ((keys[0:1] == item) | (keys[1:2] == item)).astype(BF16)
        first = ((earlier[0:1] == item) | (earlier[1:2] == item)).astype(BF16)
        rows1 = dot(first, got, NN)
        rows2 = dot(second, got, NN)
        spread = jnp.concatenate(
            [
                jnp.where(iota((128, 128), 0) == INFO, float(ROWS), 0.0) + (iota((128, 128), 0) == INFO + 1).astype(F32),
                jnp.where(iota((128, 128), 0) == INFO + 1, 2.0, 0.0) + (iota((128, 128), 0) == INFO + 5).astype(F32),
                (iota((128, 128), 0) == INFO + 3).astype(F32),
                (iota((128, 128), 0) == INFO + 4).astype(F32),
                (iota((128, 128), 0) == INFO + 5).astype(F32),
            ],
            axis=1,
        )
        known = dot(rows2.astype(BF16), spread.astype(BF16), NN)
        source, place, label, slot, half = [known[:, 128 * i : 128 * i + 128] for i in range(5)]
        number = iota((1, total), 1).astype(F32)
        picks = ((number == source[:, 0:1] + 8.0) | (number == source[:, 0:1] + 20.0)).astype(BF16)
        angle = dot(picks, got, NN)
        angle = jnp.where((half > 0.5) == odd, angle, pltpu.roll(angle, PIX, 1))
        turned1, turned2 = pltpu.roll(rows1, PIX, 1), pltpu.roll(rows2, PIX, 1)
        red = jnp.where(odd, turned1, rows1)
        green = jnp.where(odd, rows1, turned1)
        blue = jnp.where(odd, turned2, rows2)
        own = jnp.where(colour == 0, red, jnp.where(colour == 1, green, blue))
        cross = SKEW * jnp.where(colour == 0, blue - green, jnp.where(colour == 1, red - blue, green - red))
        grey = (red + green + blue) * (1.0 / 3.0)
        square = angle * angle
        sin, cos = sin_cos(angle, square)
        valid = (colour < 3) & (lane_half == odd)
        shade = own - grey
        attacked = jnp.where(valid, grey + cos * shade + sin * cross, 0.0).reshape(GROUP // 2, 8, 128)
        turning = jnp.where(valid, cos * cross - sin * shade, 0.0).reshape(GROUP // 2, 8, 128)
        att_ref[...] = attacked + pltpu.roll(attacked, 4, 1)
        turn_ref[...] = turning + pltpu.roll(turning, 4, 1)
        score = jnp.where(lane < class_ref.shape[1], PIX * (1.0 / class_ref.shape[1] - (lane.astype(F32) == label).astype(F32)), 0.0)
        pg_ref[...] = dot(
            score[:, 0 : class_ref.shape[1]], class_ref[...], NT, lax.Precision.HIGHEST
        ).reshape(GROUP // 2, 8, 128)
        place_ref[...] = jnp.where(item < owned, place, -1.0).reshape(GROUP // 2, 8, 128)
        slot_ref[...] = jnp.where((item >= owned) & (item < item_count.astype(F32)), slot, -1.0).reshape(GROUP // 2, 8, 128)

    def convolve(forward):
        for f in range(4):
            columns = slice(256 * f, 256 * f + 256)
            if forward:
                left = jnp.concatenate(
                    [act_ref[tap % 3, 32 * (tap // 3) : 32 * (tap // 3) + 256, columns] for tap in range(9)], axis=1
                )
                mix_ref[:, columns] = dot(left, weight_ref[f].reshape(2304, 256), NN)
            else:
                result = None
                for tap in range(9):
                    start = 32 * (2 - tap // 3)
                    part = dot(act_ref[2 - tap % 3, start : start + 256, columns], weight_ref[f, tap], NT)
                    result = part if result is None else result + part
                mix_ref[:, columns] = result

    x_of = iota((CHUNK, 8, 128), 1)

    def put(y, number, value):
        value = value.reshape(CHUNK, 8, 128)
        less = jnp.where(x_of == 0, 0.0, pltpu.roll(value, 1, 1))
        more = jnp.where(x_of == 7, 0.0, pltpu.roll(value, 7, 1))
        rows = pl.ds(pl.multiple_of(32 * y + 32, 32), 32)
        for which, part in enumerate((less, value, more)):
            act_ref[which, rows, 128 * number : 128 * number + 128] = part.reshape(32, 128).astype(BF16)

    def silu_parts(h):
        t = jnp.tanh(h)
        one = 1.0 + t
        return h * one, one, t

    def row_block(y):
        return pl.ds(pl.multiple_of(32 * y, 32), 32)

    def chunk(number, base):
        first_item = base + number * CHUNK
        needs_grad = first_item < owned_count
        pair = number * (CHUNK // 2)
        columns = []
        for u in range(CHUNK // 2):
            value = att_ref[pair + u]
            upper = value.astype(BF16).astype(F32)
            value = jnp.where(iota((8, 128), 0) < 4, upper, value - upper)
            taps = [
                jnp.where(tap_mask(tap // 3 - 1, tap % 3 - 1), shifted(value, 8 * (tap // 3 - 1) + tap % 3 - 1), 0.0)
                for tap in range(9)
            ]
            columns.append(jnp.concatenate(taps + taps, axis=0))
        patches = jnp.concatenate(columns, axis=1).astype(BF16)
        lift_ref[...] = dot(patches, forward_ref[...], TN).reshape(CHUNK, 8, 8, 384)

        def lift_row(y, _):
            lifted = lift_ref[:, y].reshape(32, 384)
            g, p, q = lifted[:, 0:128], lifted[:, 128:256], lifted[:, 256:384]
            minus, plus = (p - q) * HALF, (p + q) * HALF
            hues = [g + p, g + minus, g - q, g - plus, g - p, g - minus, g + q, g + plus]
            activated = []
            for k, h in enumerate(hues):
                value, one, t = silu_parts(h)
                slope_ref[row_block(y), 128 * k : 128 * k + 128] = one * (1.0 + h * (1.0 - t))
                activated.append(value)
            for number, part in enumerate(hue_fourier(activated)):
                put(y, number, part)
            return 0

        lax.fori_loop(0, 8, lift_row, 0)
        convolve(True)
        pool_ref[...] = jnp.zeros_like(pool_ref)
        slopes = [pg_ref[pair + t // 2][4 * (t % 2) : 4 * (t % 2) + 1] for t in range(CHUNK)]
        spread = jnp.concatenate([jnp.broadcast_to(s, (8, 128)) for s in slopes], axis=0) * (0.5 / 512.0)

        def mixed_row(grad, y, _):
            parts = [mix_ref[row_block(y), 128 * k : 128 * k + 128] for k in range(8)]
            summed, slope = None, []
            for h in hue_inverse(parts):
                value, one, t = silu_parts(h)
                summed = value if summed is None else summed + value
                if grad:
                    slope.append(one * (1.0 + h * (1.0 - t)) * spread)
            pool_ref[...] += summed
            if grad:
                for number, part in enumerate(hue_fourier(slope)):
                    put(y, number, part)
            return 0

        @pl.when(jnp.logical_not(needs_grad))
        def _():
            lax.fori_loop(0, 8, functools.partial(mixed_row, False), 0)

        @pl.when(needs_grad)
        def _():
            lax.fori_loop(0, 8, functools.partial(mixed_row, True), 0)

        pooled = jnp.sum(pool_ref[...].reshape(CHUNK, 8, 128), axis=1)
        gains = jnp.concatenate(slopes, axis=0)
        margin = jnp.sum(pooled * gains, axis=1, keepdims=True) * (-1.0 / (PIX * 512.0))
        lane_number = iota((1, 128), 1).astype(F32)
        for t in range(CHUNK):
            at = slot_ref[pair + t // 2][4 * (t % 2) : 4 * (t % 2) + 1]
            margin_ref[...] += jnp.where(lane_number == at, margin[t : t + 1], 0.0)

        @pl.when(needs_grad)
        def _():
            convolve(False)

            def back_row(y, _):
                parts = [mix_ref[row_block(y), 128 * k : 128 * k + 128] for k in range(8)]
                grads = [
                    part * slope_ref[row_block(y), 128 * k : 128 * k + 128] for k, part in enumerate(hue_inverse(parts))
                ]
                s = [grads[i] + grads[i + 4] for i in range(4)]
                d = [grads[i] - grads[i + 4] for i in range(4)]
                minus, plus = (d[1] - d[3]) * HALF, (d[1] + d[3]) * HALF
                g = (s[0] + s[2]) + (s[1] + s[3])
                p = d[0] + minus
                q = -d[2] - plus
                for i, value in enumerate((g, p, q)):
                    upper = value.astype(BF16).astype(F32)
                    lower = value - upper
                    for place, part in ((i, upper), (i + 3, lower), (i + 6, upper)):
                        back_ref[:, y, :, 128 * place : 128 * place + 128] = part.reshape(CHUNK, 8, 128)
                return 0

            lax.fori_loop(0, 8, back_row, 0)
            gradient = dot(backward_ref[...], back_ref[...].reshape(256, 1152).astype(BF16), NT)
            where_lane = iota((16, 128), 1)
            number_of = (2 * iota((16, 128), 0) + where_lane // PIX).astype(F32)
            for u in range(CHUNK // 2):
                colour_grad = jnp.zeros((8, 128), F32)
                for tap in range(9):
                    dy, dx = tap // 3 - 1, tap % 3 - 1
                    part = gradient[8 * tap : 8 * tap + 8, 128 * u : 128 * u + 128]
                    colour_grad += jnp.where(tap_mask(-dy, -dx), shifted(part, -8 * dy - dx), 0.0)
                angle_grad = jnp.sum(colour_grad * turn_ref[pair + u], axis=0, keepdims=True)
                turned = pltpu.roll(jnp.broadcast_to(angle_grad, (8, 128)), PIX, 1)[0:1]
                places = place_ref[pair + u]
                for t in range(2):
                    chosen = jnp.where((iota((1, 128), 1) >= PIX) == (t == 1), angle_grad, turned)
                    same = number_of == places[4 * t : 4 * t + 1]
                    sum_ref[...] += jnp.where(same, chosen, 0.0)
                    count_ref[...] += same.astype(F32)

    def run_group(group, _):
        gather(group)

        @pl.when(group == 0)
        def _():
            copy.wait()

        base = group * GROUP
        chunks = jnp.minimum((item_count - base + CHUNK - 1) // CHUNK, GROUP // CHUNK)
        lax.fori_loop(0, chunks, lambda number, _: (chunk(number, base), 0)[1], 0)
        return 0

    groups = jnp.maximum((item_count + GROUP - 1) // GROUP, 1)
    lax.fori_loop(0, groups, run_group, 0)
    grad_ref[...] = (sum_ref[...] / jnp.maximum(count_ref[...], 1.0))[0 : grad_ref.shape[0]]


def sin_cos(angle, square):
    sin = -1.0 / 39916800.0
    for coefficient in (1.0 / 362880.0, -1.0 / 5040.0, 1.0 / 120.0, -1.0 / 6.0, 1.0):
        sin = sin * square + coefficient
    cos = 1.0 / 479001600.0
    for coefficient in (-1.0 / 3628800.0, 1.0 / 40320.0, -1.0 / 720.0, 1.0 / 24.0, -0.5, 1.0):
        cos = cos * square + coefficient
    return sin * angle, cos


def vmem(count):
    return [pl.BlockSpec(memory_space=pltpu.VMEM) for _ in range(count)]


def shards(
    tiles, tile_slide, tile_mask, tile_label, attack_field, lift_weight, group_weight, class_weight
):
    devices = lax.axis_size("tiles")
    field = attack_field.reshape(-1, 128)
    slides = attack_field.shape[0] // PIX
    message = pl.pallas_call(
        functools.partial(pack_kernel, slides),
        out_shape=jax.ShapeDtypeStruct((devices, ROWS, 128), BF16),
        in_specs=[pl.BlockSpec(memory_space=pltpu.SMEM)] * 3 + vmem(2),
        out_specs=pl.BlockSpec(memory_space=pltpu.VMEM),
        name="pack",
    )(tile_slide, tile_mask, tile_label, tiles, field)
    got = lax.all_to_all(message, "tiles", split_axis=0, concat_axis=0, tiled=True)
    weights, forward, backward = pl.pallas_call(
        weight_kernel,
        grid=(9,),
        out_shape=(
            jax.ShapeDtypeStruct((4, 9, 256, 256), BF16),
            jax.ShapeDtypeStruct((144, 384), BF16),
            jax.ShapeDtypeStruct((80, 1152), BF16),
        ),
        in_specs=[
            pl.BlockSpec((8, 1, 128, 128), lambda tap: (0, tap, 0, 0)),
            pl.BlockSpec((9, 3, 128), lambda tap: (0, 0, 0)),
        ],
        out_specs=(
            pl.BlockSpec((4, 1, 256, 256), lambda tap: (0, tap, 0, 0)),
            pl.BlockSpec((144, 384), lambda tap: (0, 0)),
            pl.BlockSpec((80, 1152), lambda tap: (0, 0)),
        ),
        compiler_params=pltpu.CompilerParams(dimension_semantics=("arbitrary",), vmem_limit_bytes=16 * 2**20),
        cost_estimate=pl.CostEstimate(flops=10_000_000, bytes_accessed=7_000_000, transcendentals=0),
        name="weights",
    )(group_weight, lift_weight)
    total = devices * ROWS
    margins, attack_grad = pl.pallas_call(
        main_kernel,
        out_shape=(jax.ShapeDtypeStruct((1, 128), F32), jax.ShapeDtypeStruct(field.shape, F32)),
        in_specs=vmem(1) + [pl.BlockSpec(memory_space=pl.ANY)] + vmem(3),
        out_specs=tuple(vmem(2)),
        scratch_shapes=[
            pltpu.VMEM((4, 9, 256, 256), BF16),
            pltpu.VMEM((8, total), F32),
            pltpu.VMEM((GROUP // 2, 8, 128), F32),
            pltpu.VMEM((GROUP // 2, 8, 128), F32),
            pltpu.VMEM((GROUP // 2, 8, 128), F32),
            pltpu.VMEM((GROUP // 2, 8, 128), F32),
            pltpu.VMEM((GROUP // 2, 8, 128), F32),
            pltpu.VMEM((CHUNK, 8, 8, 384), F32),
            pltpu.VMEM((256, 1024), F32),
            pltpu.VMEM((3, 320, 1024), BF16),
            pltpu.VMEM((256, 1024), F32),
            pltpu.VMEM((32, 128), F32),
            pltpu.VMEM((CHUNK, 8, 8, 1152), F32),
            pltpu.VMEM((16, 128), F32),
            pltpu.VMEM((16, 128), F32),
            pltpu.SemaphoreType.DMA,
        ],
        compiler_params=pltpu.CompilerParams(vmem_limit_bytes=40 * 2**20),
        cost_estimate=pl.CostEstimate(flops=4_000_000_000, bytes_accessed=6_000_000, transcendentals=2_000_000),
        name="attack",
    )(got, weights, forward, backward, class_weight)
    return (margins[0, 0 : tile_slide.shape[0]], attack_grad.reshape(-1))


def solution(mesh):
    return jax.shard_map(
        shards,
        mesh=mesh,
        in_specs=(
            P(None, ("groups", "tiles")),
            P(("groups", "tiles")),
            P(("groups", "tiles")),
            P(("groups", "tiles")),
            P(("groups", "tiles")),
            P(),
            P(),
            P(),
        ),
        out_specs=(P(("groups", "tiles")), P(("groups", "tiles"))),
        check_vma=False,
    )
```

```python
import functools
import math

import jax
import jax.numpy as jnp
from jax import lax
from jax.experimental import pallas as pl
from jax.experimental.pallas import tpu as pltpu
from jax.sharding import PartitionSpec as P

F32 = jnp.float32
BF16 = jnp.bfloat16
PIX = 64
ROWS = 32
INFO = 64
SLOTS = 4
GROUP = 8
SKEW = 1.0 / math.sqrt(3.0)
HALF = math.sqrt(0.5)


def iota(shape, axis):
    return lax.broadcasted_iota(jnp.int32, shape, axis)


def dot(a, b, dims, precision=None):
    return lax.dot_general(a, b, (dims, ((), ())), precision=precision, preferred_element_type=F32)


NN = ((1,), (0,))
NT = ((1,), (1,))
TN = ((0,), (0,))


def hue_fourier(x):
    s = [x[i] + x[i + 4] for i in range(4)]
    d = [x[i] - x[i + 4] for i in range(4)]
    e, o = s[0] + s[2], s[1] + s[3]
    dm, dp = (d[1] - d[3]) * HALF, (d[1] + d[3]) * HALF
    return [e + o, e - o, d[0] + dm, -d[2] - dp, s[0] - s[2], s[3] - s[1], d[0] - dm, d[2] - dp]


def hue_inverse(c):
    f0, f4, r1, i1, r2, i2, r3, i3 = c
    a, b = f0 + f4, f0 - f4
    s0, s2, s1, s3 = a + r2, a - r2, b - i2, b + i2
    d0, d2 = r1 + r3, i3 - i1
    p, q = (r1 - r3) * HALF, (i1 + i3) * HALF
    d1, d3 = p - q, -p - q
    s, d = (s0, s1, s2, s3), (d0, d1, d2, d3)
    return [s[k] + d[k] for k in range(4)] + [s[k] - d[k] for k in range(4)]


def pack_kernel(slides, slide_ref, mask_ref, label_ref, tiles_ref, field_ref, out_ref):
    lane = iota((1, 128), 1)
    left = lane < PIX
    tiles = tiles_ref[...].astype(F32)
    rows, parts = [], []
    for slot in range(4):
        part = tiles[:, 128 * (slot // 2) : 128 * (slot // 2) + 128]
        turned = pltpu.roll(part, PIX, 1)
        low, high = (part, turned) if slot % 2 == 0 else (turned, part)
        slide = slide_ref[slot]
        owner = slide // slides
        place = slide - owner * slides
        facts = [owner, place // 2, mask_ref[slot], label_ref[slot], slot, place % 2]
        info = jnp.zeros((1, 128), jnp.int32)
        for number, fact in enumerate(facts):
            info = jnp.where(lane == INFO + number, fact, info)
        rows.append(jnp.where(left, low[0:1], high[1:2]))
        rows.append(jnp.where(left, low[2:3], info.astype(F32)))
    rows = jnp.concatenate(rows, axis=0)
    field = field_ref[...]
    upper = field.astype(BF16).astype(F32)
    rest = jnp.concatenate([upper, field - upper], axis=0)
    at = (iota((8, 128), 1) == INFO + 6) & (iota((8, 128), 0) % 2 == 1)
    for target in range(out_ref.shape[0]):
        slot_rows = jnp.where(at, float(target), rows)
        out_ref[target] = jnp.concatenate([slot_rows, rest], axis=0).astype(BF16)


def weight_kernel(
    weight_hbm, lift_hbm,
    ahead_hbm, back_hbm, forward_ref, backward_ref,
    raw, lift_ref, ahead, back, in_sem, lift_sem, out_sem,
):
    def fetch(tap):
        return pltpu.make_async_copy(weight_hbm.at[:, tap], raw.at[tap], in_sem.at[tap])

    def store(tap):
        return (
            pltpu.make_async_copy(ahead.at[tap], ahead_hbm.at[tap], out_sem.at[0, tap]),
            pltpu.make_async_copy(back.at[tap], back_hbm.at[tap], out_sem.at[1, tap]),
        )

    lift_copy = pltpu.make_async_copy(lift_hbm, lift_ref, lift_sem)
    lift_copy.start()
    for tap in range(9):
        fetch(tap).start()
    lift_copy.wait()

    both, single = [], []
    for tap in range(9):
        lift = lift_ref[tap]
        l0, l1, l2 = lift[0:1], lift[1:2], lift[2:3]
        grey = (l0 + l1 + l2) * (1.0 / 3.0)
        zero = jnp.zeros((1, 128), F32)
        columns = (
            [grey] * 3,
            [l0 - grey, l1 - grey, l2 - grey],
            [(l1 - l2) * SKEW, (l2 - l0) * SKEW, (l0 - l1) * SKEW],
        )
        both.append(jnp.concatenate([jnp.concatenate([*c, zero, *c, zero], axis=0) for c in columns], axis=1))
        single.append(jnp.concatenate([jnp.concatenate([*c, *[zero] * 5], axis=0) for c in columns], axis=1))
    both = jnp.concatenate(both, axis=0) * 0.5
    upper = both.astype(BF16).astype(F32)
    forward_ref[...] = jnp.concatenate([upper, both - upper], axis=0).astype(BF16)
    single = jnp.concatenate(single + [jnp.zeros((8, 384), F32)], axis=0)
    upper = single.astype(BF16).astype(F32)
    backward_ref[...] = jnp.concatenate([upper, upper, single - upper], axis=1).astype(BF16)

    def work(tap, _):
        fetch(tap).wait()
        for block in range(0, 128, 32):
            rows = slice(block, block + 32)
            f0, f4, r1, i1, r2, i2, r3, i3 = hue_fourier([raw[tap, k, rows, :].astype(F32) for k in range(8)])
            parts = [f0 * 0.0625, f4 * 0.0625]
            for re, im in ((r1, i1), (r2, i2), (r3, i3)):
                re, im = re * 0.125, im * 0.125
                parts += [re, -im, im]
            for number, part in enumerate(parts):
                ahead[tap, number, rows, :] = part.astype(BF16)
        for number in range(11):
            back[tap, number] = ahead[tap, number].T
        for copy in store(tap):
            copy.start()
        return 0

    lax.fori_loop(0, 9, work, 0)
    for tap in range(9):
        for copy in store(tap):
            copy.wait()


def tap_mask(dy, dx):
    lane = iota((1, 128), 1)
    x, y = lane % 8 + dx, (lane // 8) % 8 + dy
    return (x >= 0) & (x < 8) & (y >= 0) & (y < 8)


def shifted(value, by):
    return value if by % 128 == 0 else pltpu.roll(value, (-by) % 128, 1)


def main_kernel(
    got_ref, ahead_hbm, back_hbm, forward_ref, backward_ref, class_hbm,
    margin_ref, grad_ref,
    ahead_ref, turned_ref, class_ref, key_ref, att_ref, turn_ref, pg_ref, place_ref, live_ref,
    lift_ref, slope_ref, act_own, act_here, act_back, mix_own, mix_here, mix_back, back_ref, sum_ref, count_ref, sems,
):
    total = got_ref.shape[0] * ROWS
    ahead_copy = pltpu.make_async_copy(ahead_hbm, ahead_ref, sems.at[0])
    back_copy = pltpu.make_async_copy(back_hbm, turned_ref, sems.at[1])
    class_copy = pltpu.make_async_copy(class_hbm, class_ref, sems.at[2])
    class_copy.start()
    ahead_copy.start()
    back_copy.start()
    got = got_ref[...].reshape(total, 128)

    picker = (iota((8, 128), 1) == INFO + iota((8, 128), 0)).astype(BF16)
    facts = dot(picker, got, NT)
    spot = iota((1, total), 1)
    within = spot % ROWS
    is_slot = (within < 8) & (within % 2 == 1)
    me = facts[6:7]
    mine = is_slot & (facts[2:3] > 0.5) & (facts[0:1] == me)
    here = is_slot & ((spot // ROWS).astype(F32) == me)
    marks = jnp.broadcast_to(mine.astype(F32), (8, total))
    before = (iota((128, 128), 0) < iota((128, 128), 1)).astype(BF16)
    carry, ranks = jnp.zeros((8, 1), F32), []
    for block in range(total // 128):
        part = marks[:, block * 128 : block * 128 + 128]
        ranks.append(dot(part.astype(BF16), before, NN) + carry)
        carry = carry + jnp.sum(part, axis=1, keepdims=True)
    ranks = jnp.concatenate(ranks, axis=1)
    owned = carry[0:1]
    key_mine = jnp.where(mine, ranks[0:1] + float(SLOTS), -1.0)
    key_here = jnp.where(here, (within // 2).astype(F32), -1.0)
    key_ref[...] = jnp.concatenate([key_mine, key_here, jnp.full((6, total), -1.0, F32)], axis=0)
    owned_count = jnp.sum(owned).astype(jnp.int32)

    sum_ref[...] = jnp.zeros_like(sum_ref)
    count_ref[...] = jnp.zeros_like(count_ref)
    for ref in (act_own, act_here, act_back):
        ref[:, 0:16, :] = jnp.zeros((3, 16, 1024), BF16)
        ref[:, 144:160, :] = jnp.zeros((3, 16, 1024), BF16)

    def gather(first_item, pairs, at):
        height = pairs * 8
        lane = iota((height, 128), 1)
        odd = iota((height, 128), 0) % 8 >= 4
        colour = iota((height, 128), 0) % 4
        item = (first_item + 2 * (iota((height, 1), 0) // 8) + (iota((height, 1), 0) % 8) // 4).astype(F32)
        keys = key_ref[...]
        earlier = pltpu.roll(keys, total - 1, 1)
        second = ((keys[0:1] == item) | (keys[1:2] == item)).astype(BF16)
        first = ((earlier[0:1] == item) | (earlier[1:2] == item)).astype(BF16)
        rows2 = dot(second, got, NN)
        rows1 = dot(first, got, NN)
        owner, step, live, label, half = [rows2[:, INFO + i : INFO + i + 1] for i in (0, 1, 2, 3, 5)]
        source = owner * float(ROWS) + step
        number = iota((1, total), 1).astype(F32)
        picks = ((number == source + 8.0) | (number == source + 20.0)).astype(BF16)
        angle = dot(picks, got, NN)
        angle = jnp.where((half > 0.5) == odd, angle, pltpu.roll(angle, PIX, 1))
        turned1, turned2 = pltpu.roll(rows1, PIX, 1), pltpu.roll(rows2, PIX, 1)
        red = jnp.where(odd, turned1, rows1)
        green = jnp.where(odd, rows1, turned1)
        blue = jnp.where(odd, turned2, rows2)
        own = jnp.where(colour == 0, red, jnp.where(colour == 1, green, blue))
        cross = SKEW * jnp.where(colour == 0, blue - green, jnp.where(colour == 1, red - blue, green - red))
        grey = (red + green + blue) * (1.0 / 3.0)
        sin, cos = sin_cos(angle, angle * angle)
        valid = (colour < 3) & ((lane >= PIX) == odd)
        shade = own - grey
        attacked = jnp.where(valid, grey + cos * shade + sin * cross, 0.0).reshape(pairs, 8, 128)
        turning = jnp.where(valid, cos * cross - sin * shade, 0.0).reshape(pairs, 8, 128)
        classes = class_ref.shape[0]
        score = jnp.where(lane < classes, PIX * (1.0 / classes - (lane.astype(F32) == label).astype(F32)), 0.0)
        gain = dot(score[:, 0:classes], class_ref[...], NN, lax.Precision.HIGHEST)
        place = jnp.where((item >= SLOTS) & (item < owned + SLOTS), 2.0 * step + half, -1.0)
        spots = pl.ds(at, pairs)
        att_ref[spots] = attacked + pltpu.roll(attacked, 4, 1)
        turn_ref[spots] = turning + pltpu.roll(turning, 4, 1)
        pg_ref[spots] = gain.reshape(pairs, 8, 128)
        place_ref[spots] = jnp.broadcast_to(place, (height, 128)).reshape(pairs, 8, 128)
        live_ref[spots] = jnp.broadcast_to(live, (height, 128)).reshape(pairs, 8, 128)

    x_of = iota((2, 8, 128), 1)

    def put(act, y, number, value):
        value = value.reshape(2, 8, 128)
        less = jnp.where(x_of == 0, 0.0, pltpu.roll(value, 1, 1))
        more = jnp.where(x_of == 7, 0.0, pltpu.roll(value, 7, 1))
        for which, part in enumerate((less, value, more)):
            act[which, 16 * y + 16 : 16 * y + 32, 128 * number : 128 * number + 128] = part.reshape(16, 128).astype(BF16)

    def lift(pair, act, slope):
        def start():
            value = att_ref[pair]
            upper = value.astype(BF16).astype(F32)
            value = jnp.where(iota((8, 128), 0) < 4, upper, value - upper)
            taps = [
                jnp.where(tap_mask(tap // 3 - 1, tap % 3 - 1), shifted(value, 8 * (tap // 3 - 1) + tap % 3 - 1), 0.0)
                for tap in range(9)
            ]
            patches = jnp.concatenate(taps + taps, axis=0).astype(BF16)
            lift_ref[...] = dot(patches, forward_ref[...], TN).reshape(2, 8, 8, 384)

        def line(y):
            lifted = lift_ref[:, y].reshape(16, 384)
            g, p, q = lifted[:, 0:128], lifted[:, 128:256], lifted[:, 256:384]
            minus, plus = (p - q) * HALF, (p + q) * HALF
            hues = [g + p, g + minus, g - q, g - plus, g - p, g - minus, g + q, g + plus]
            activated = []
            for k, h in enumerate(hues):
                t = jnp.tanh(h)
                one = 1.0 + t
                if slope is not None:
                    slope_ref[slope, 16 * y : 16 * y + 16, 128 * k : 128 * k + 128] = one * (1.0 + h * (1.0 - t))
                activated.append(h * one)
            for number, part in enumerate(hue_fourier(activated)):
                put(act, y, number, part)

        return [start] + [functools.partial(line, y) for y in range(8)]

    def convolve(act, out, forward):
        def part(f):
            columns = slice(256 * f, 256 * f + 256)
            left, right = [], []
            for tap in range(9):
                dy, dx = (tap // 3, tap % 3) if forward else (2 - tap // 3, 2 - tap % 3)
                left.append(act[dx, 16 * dy : 16 * dy + 128, columns])
                weights = ahead_ref if forward else turned_ref
                if f == 0:
                    zero = jnp.zeros((128, 128), BF16)
                    square = ((weights[tap, 0], zero), (zero, weights[tap, 1]))
                else:
                    re, minus, plus = [weights[tap, 3 * f - 1 + i] for i in range(3)]
                    square = ((re, minus), (plus, re)) if forward else ((re, plus), (minus, re))
                right += [jnp.concatenate(pieces, axis=1) for pieces in square]
            out[:, columns] = dot(jnp.concatenate(left, axis=1), jnp.concatenate(right, axis=0), NN)

        return [functools.partial(part, f) for f in range(4)]

    def gains(pair):
        return [pg_ref[pair][4 * t : 4 * t + 1] for t in range(2)]

    def slopes(pair, mix):
        spread = jnp.concatenate([jnp.broadcast_to(g, (8, 128)) for g in gains(pair)], axis=0) * (0.5 / 512.0)

        def line(y):
            parts = [mix[16 * y : 16 * y + 16, 128 * k : 128 * k + 128] for k in range(8)]
            slope = []
            for h in hue_inverse(parts):
                t = jnp.tanh(h)
                slope.append((1.0 + t) * (1.0 + h * (1.0 - t)) * spread)
            for number, part in enumerate(hue_fourier(slope)):
                put(act_back, y, number, part)

        return [functools.partial(line, y) for y in range(8)]

    def pool(pair, mix):
        sums = []

        def line(y):
            parts = [mix[16 * y : 16 * y + 16, 128 * k : 128 * k + 128] for k in range(8)]
            values = [h * (1.0 + jnp.tanh(h)) for h in hue_inverse(parts)]
            while len(values) > 1:
                values = [a + b for a, b in zip(values[::2], values[1::2])]
            sums[:] = [sums[0] + values[0]] if sums else values

        def finish():
            pooled = jnp.sum(sums[0].reshape(2, 8, 128), axis=1)
            gain = jnp.concatenate(gains(pair), axis=0)
            margin = jnp.sum(pooled * gain, axis=1, keepdims=True) * (-1.0 / (PIX * 512.0))
            live = live_ref[pair]
            return [margin[t : t + 1] * live[4 * t : 4 * t + 1] for t in range(2)]

        return [functools.partial(line, y) for y in range(8)], finish

    def back(pair, slope):
        def line(y):
            parts = [mix_back[16 * y : 16 * y + 16, 128 * k : 128 * k + 128] for k in range(8)]
            grads = [
                part * slope_ref[slope, 16 * y : 16 * y + 16, 128 * k : 128 * k + 128]
                for k, part in enumerate(hue_inverse(parts))
            ]
            s = [grads[i] + grads[i + 4] for i in range(4)]
            d = [grads[i] - grads[i + 4] for i in range(4)]
            minus, plus = (d[1] - d[3]) * HALF, (d[1] + d[3]) * HALF
            for i, value in enumerate(((s[0] + s[2]) + (s[1] + s[3]), d[0] + minus, -d[2] - plus)):
                upper = value.astype(BF16).astype(F32)
                for place, part in ((i, upper), (i + 3, value - upper), (i + 6, upper)):
                    back_ref[:, y, :, 128 * place : 128 * place + 128] = part.reshape(2, 8, 128)

        def finish():
            gradient = dot(backward_ref[...], back_ref[...].reshape(128, 1152).astype(BF16), NT)
            number_of = (2 * iota((16, 128), 0) + iota((16, 128), 1) // PIX).astype(F32)
            colour_grad = jnp.zeros((8, 128), F32)
            for tap in range(9):
                dy, dx = tap // 3 - 1, tap % 3 - 1
                part = gradient[8 * tap : 8 * tap + 8]
                colour_grad += jnp.where(tap_mask(-dy, -dx), shifted(part, -8 * dy - dx), 0.0)
            angle_grad = jnp.sum(colour_grad * turn_ref[pair], axis=0, keepdims=True)
            turned = pltpu.roll(jnp.broadcast_to(angle_grad, (8, 128)), PIX, 1)[0:1]
            places = place_ref[pair]
            for t in range(2):
                chosen = jnp.where((iota((1, 128), 1) >= PIX) == (t == 1), angle_grad, turned)
                same = number_of == places[4 * t : 4 * t + 1]
                sum_ref[...] += jnp.where(same, chosen, 0.0)
                count_ref[...] += same.astype(F32)

        return [functools.partial(line, y) for y in range(8)] + [finish]

    def together(*lists):
        longest = max(len(steps) for steps in lists)
        for place in range(longest):
            for steps in lists:
                for number in range(len(steps) * place // longest, len(steps) * (place + 1) // longest):
                    steps[number]()

    first_own = SLOTS // 2
    class_copy.wait()
    gather(0, (SLOTS + GROUP) // 2, 0)
    together(lift(first_own, act_own, 0))
    ahead_copy.wait()
    together(convolve(act_own, mix_own, True), lift(0, act_here, None))
    together(convolve(act_here, mix_here, True), slopes(first_own, mix_own))
    back_copy.wait()
    together(convolve(act_back, mix_back, False), lift(1, act_here, None))
    lines, margins0 = pool(0, mix_here)
    together(convolve(act_here, mix_own, True), lines, lift(first_own + 1, act_own, 1))
    margins = margins0()

    pairs = (owned_count + 1) // 2

    def more(pair, _):
        together(convolve(act_own, mix_here, True), back(first_own + pair - 1, (pair + 1) % 2))
        together(slopes(first_own + pair, mix_here))
        after = pair + 1

        @pl.when((after % (GROUP // 2) == 0) & (after < pairs))
        def _():
            gather(SLOTS + 2 * after, GROUP // 2, first_own + after)

        together(convolve(act_back, mix_back, False), lift(first_own + after, act_own, after % 2))
        return 0

    lax.fori_loop(1, pairs, more, 0)
    lines, margins1 = pool(1, mix_own)
    last = jnp.maximum(pairs - 1, 0)
    together(back(first_own + last, last % 2), lines)
    margins += margins1()
    lane1 = iota((1, 128), 1)
    result = jnp.zeros((1, 128), F32)
    for number, margin in enumerate(margins):
        result = jnp.where(lane1 == number, margin, result)
    margin_ref[...] = result[0, 0 : margin_ref.shape[0]]
    grad_ref[...] = (sum_ref[...] / jnp.maximum(count_ref[...], 1.0))[0 : grad_ref.shape[0]]


def sin_cos(angle, square):
    sin = -1.0 / 39916800.0
    for coefficient in (1.0 / 362880.0, -1.0 / 5040.0, 1.0 / 120.0, -1.0 / 6.0, 1.0):
        sin = sin * square + coefficient
    cos = 1.0 / 479001600.0
    for coefficient in (-1.0 / 3628800.0, 1.0 / 40320.0, -1.0 / 720.0, 1.0 / 24.0, -0.5, 1.0):
        cos = cos * square + coefficient
    return sin * angle, cos


def vmem(count):
    return [pl.BlockSpec(memory_space=pltpu.VMEM) for _ in range(count)]


def in_hbm(array):
    return pltpu.with_memory_space_constraint(array, pltpu.HBM)


def shards(
    tiles, tile_slide, tile_mask, tile_label, attack_field, lift_weight, group_weight, class_weight
):
    devices = lax.axis_size("tiles")
    field = attack_field.reshape(-1, 128)
    slides = attack_field.shape[0] // PIX
    message = pl.pallas_call(
        functools.partial(pack_kernel, slides),
        out_shape=jax.ShapeDtypeStruct((devices, ROWS, 128), BF16),
        in_specs=[pl.BlockSpec(memory_space=pltpu.SMEM)] * 3 + vmem(2),
        out_specs=pl.BlockSpec(memory_space=pltpu.VMEM),
        name="pack",
    )(tile_slide, tile_mask, tile_label, tiles, field)
    got = lax.all_to_all(message, "tiles", split_axis=0, concat_axis=0, tiled=True)
    hbm = pl.BlockSpec(memory_space=pltpu.HBM)
    ahead, turned, forward, backward = pl.pallas_call(
        weight_kernel,
        out_shape=(
            pltpu.HBM((9, 11, 128, 128), BF16),
            pltpu.HBM((9, 11, 128, 128), BF16),
            jax.ShapeDtypeStruct((144, 384), BF16),
            jax.ShapeDtypeStruct((80, 1152), BF16),
        ),
        in_specs=[hbm, hbm],
        out_specs=(hbm, hbm, *vmem(2)),
        scratch_shapes=[
            pltpu.VMEM((9, 8, 128, 128), BF16),
            pltpu.VMEM((9, 3, 128), F32),
            pltpu.VMEM((9, 11, 128, 128), BF16),
            pltpu.VMEM((9, 11, 128, 128), BF16),
            pltpu.SemaphoreType.DMA((9,)),
            pltpu.SemaphoreType.DMA,
            pltpu.SemaphoreType.DMA((2, 9)),
        ],
        compiler_params=pltpu.CompilerParams(vmem_limit_bytes=16 * 2**20),
        cost_estimate=pl.CostEstimate(flops=10_000_000, bytes_accessed=9_000_000, transcendentals=0),
        name="weights",
    )(in_hbm(group_weight), in_hbm(lift_weight))
    total = devices * ROWS
    spots = (SLOTS + GROUP) // 2 + devices
    margins, attack_grad = pl.pallas_call(
        main_kernel,
        out_shape=(jax.ShapeDtypeStruct(tile_slide.shape, F32), jax.ShapeDtypeStruct(field.shape, F32)),
        in_specs=vmem(1) + [hbm, hbm] + vmem(2) + [hbm],
        out_specs=tuple(vmem(2)),
        scratch_shapes=[
            pltpu.VMEM((9, 11, 128, 128), BF16),
            pltpu.VMEM((9, 11, 128, 128), BF16),
            pltpu.VMEM(class_weight.shape[::-1], F32),
            pltpu.VMEM((8, total), F32),
            *[pltpu.VMEM((spots, 8, 128), F32) for _ in range(5)],
            pltpu.VMEM((2, 8, 8, 384), F32),
            pltpu.VMEM((2, 128, 1024), F32),
            *[pltpu.VMEM((3, 160, 1024), BF16) for _ in range(3)],
            *[pltpu.VMEM((128, 1024), F32) for _ in range(3)],
            pltpu.VMEM((2, 8, 8, 1152), F32),
            pltpu.VMEM((16, 128), F32),
            pltpu.VMEM((16, 128), F32),
            pltpu.SemaphoreType.DMA((3,)),
        ],
        compiler_params=pltpu.CompilerParams(vmem_limit_bytes=32 * 2**20),
        cost_estimate=pl.CostEstimate(flops=4_000_000_000, bytes_accessed=9_000_000, transcendentals=2_000_000),
        name="attack",
    )(got, in_hbm(ahead), in_hbm(turned), forward, backward, in_hbm(class_weight.T))
    return (margins, attack_grad.reshape(-1))


def solution(mesh):
    return jax.shard_map(
        shards,
        mesh=mesh,
        in_specs=(
            P(None, ("groups", "tiles")),
            P(("groups", "tiles")),
            P(("groups", "tiles")),
            P(("groups", "tiles")),
            P(("groups", "tiles")),
            P(),
            P(),
            P(),
        ),
        out_specs=(P(("groups", "tiles")), P(("groups", "tiles"))),
        check_vma=False,
    )
```

```python
import functools
import math

import jax
import jax.numpy as jnp
from jax import lax
from jax.experimental import pallas as pl
from jax.experimental.pallas import tpu as pltpu
from jax.sharding import PartitionSpec as P

F32 = jnp.float32
BF16 = jnp.bfloat16
PIX = 64
ROWS = 24
INFO = 64
SLOTS = 4
GROUP = 12
SKEW = 1.0 / math.sqrt(3.0)
HALF = math.sqrt(0.5)


def iota(shape, axis):
    return lax.broadcasted_iota(jnp.int32, shape, axis)


def dot(a, b, dims, precision=None):
    return lax.dot_general(a, b, (dims, ((), ())), precision=precision, preferred_element_type=F32)


NN = ((1,), (0,))
NT = ((1,), (1,))
TN = ((0,), (0,))


def hue_fourier(x):
    s = [x[i] + x[i + 4] for i in range(4)]
    d = [x[i] - x[i + 4] for i in range(4)]
    e, o = s[0] + s[2], s[1] + s[3]
    dm, dp = (d[1] - d[3]) * HALF, (d[1] + d[3]) * HALF
    return [e + o, e - o, d[0] + dm, -d[2] - dp, s[0] - s[2], s[3] - s[1], d[0] - dm, d[2] - dp]


def hue_inverse(c):
    f0, f4, r1, i1, r2, i2, r3, i3 = c
    a, b = f0 + f4, f0 - f4
    s0, s2, s1, s3 = a + r2, a - r2, b - i2, b + i2
    d0, d2 = r1 + r3, i3 - i1
    p, q = (r1 - r3) * HALF, (i1 + i3) * HALF
    d1, d3 = p - q, -p - q
    s, d = (s0, s1, s2, s3), (d0, d1, d2, d3)
    return [s[k] + d[k] for k in range(4)] + [s[k] - d[k] for k in range(4)]


def pack_kernel(slides, slide_ref, mask_ref, label_ref, tiles_ref, field_ref, out_ref):
    lane = iota((1, 128), 1)
    left = lane < PIX
    tiles = tiles_ref[...].astype(F32)
    rows, parts = [], []
    for slot in range(4):
        part = tiles[:, 128 * (slot // 2) : 128 * (slot // 2) + 128]
        turned = pltpu.roll(part, PIX, 1)
        low, high = (part, turned) if slot % 2 == 0 else (turned, part)
        slide = slide_ref[slot]
        owner = slide // slides
        place = slide - owner * slides
        facts = [owner, place // 2, mask_ref[slot], label_ref[slot], slot, place % 2]
        info = jnp.zeros((1, 128), jnp.int32)
        for number, fact in enumerate(facts):
            info = jnp.where(lane == INFO + number, fact, info)
        rows.append(jnp.where(left, low[0:1], high[1:2]))
        rows.append(jnp.where(left, low[2:3], info.astype(F32)))
    rows = jnp.concatenate(rows, axis=0)
    rest = jnp.concatenate([field_ref[...], jnp.zeros((4, 128), F32)], axis=0)
    at = (iota((8, 128), 1) == INFO + 6) & (iota((8, 128), 0) % 2 == 1)
    for target in range(out_ref.shape[0]):
        slot_rows = jnp.where(at, float(target), rows)
        out_ref[target] = jnp.concatenate([slot_rows, rest], axis=0).astype(BF16)


def weight_kernel(
    weight_hbm, lift_hbm, field_hbm, class_hbm,
    ahead, back_hbm, forward_ref, backward_ref, fields_ref, class_ref,
    raw, lift_ref, field_ref, back, in_sem, small_sem, out_sem,
):
    def fetch(tap):
        return pltpu.make_async_copy(weight_hbm.at[:, tap], raw.at[tap], in_sem.at[tap])

    def store(tap):
        return pltpu.make_async_copy(back.at[tap], back_hbm.at[tap], out_sem.at[tap])

    small = [
        pltpu.make_async_copy(source, target, small_sem.at[number])
        for number, (source, target) in enumerate(
            ((lift_hbm, lift_ref), (field_hbm, field_ref), (class_hbm, class_ref))
        )
    ]
    for copy in small:
        copy.start()
    for tap in range(9):
        fetch(tap).start()
    for copy in small:
        copy.wait()
    field = field_ref[...]
    upper = field.astype(BF16).astype(F32)
    fields_ref[...] = jnp.concatenate([upper, field - upper, jnp.zeros((104, 128), F32)], axis=0).astype(BF16)

    both, single = [], []
    for tap in range(9):
        lift = lift_ref[tap]
        l0, l1, l2 = lift[0:1], lift[1:2], lift[2:3]
        grey = (l0 + l1 + l2) * (1.0 / 3.0)
        zero = jnp.zeros((1, 128), F32)
        columns = (
            [grey] * 3,
            [l0 - grey, l1 - grey, l2 - grey],
            [(l1 - l2) * SKEW, (l2 - l0) * SKEW, (l0 - l1) * SKEW],
        )
        both.append(jnp.concatenate([jnp.concatenate([*c, zero, *c, zero], axis=0) for c in columns], axis=1))
        single.append(jnp.concatenate([jnp.concatenate([*c, *[zero] * 5], axis=0) for c in columns], axis=1))
    both = jnp.concatenate(both, axis=0) * 0.5
    upper = both.astype(BF16).astype(F32)
    forward_ref[...] = jnp.concatenate([upper, both - upper], axis=0).astype(BF16)
    single = jnp.concatenate(single + [jnp.zeros((8, 384), F32)], axis=0)
    upper = single.astype(BF16).astype(F32)
    backward_ref[...] = jnp.concatenate([upper, upper, single - upper], axis=1).astype(BF16)

    def work(tap, _):
        fetch(tap).wait()
        for block in range(0, 128, 32):
            rows = slice(block, block + 32)
            f0, f4, r1, i1, r2, i2, r3, i3 = hue_fourier([raw[tap, k, rows, :].astype(F32) for k in range(8)])
            parts = [f0 * 0.0625, f4 * 0.0625] + [part * 0.125 for part in (r1, i1, r2, i2, r3, i3)]
            for number, part in enumerate(parts):
                ahead[tap, number, rows, :] = part.astype(BF16)
        for number in (0, 1):
            back[tap, number] = ahead[tap, number].T
        for f in (1, 2, 3):
            back[tap, 3 * f - 1] = ahead[tap, 2 * f].T
            im = ahead[tap, 2 * f + 1].T
            back[tap, 3 * f] = -im
            back[tap, 3 * f + 1] = im
        store(tap).start()
        return 0

    lax.fori_loop(0, 9, work, 0)
    for tap in range(9):
        store(tap).wait()


def tap_mask(dy, dx):
    lane = iota((1, 128), 1)
    x, y = lane % 8 + dx, (lane // 8) % 8 + dy
    return (x >= 0) & (x < 8) & (y >= 0) & (y < 8)


def shifted(value, by):
    return value if by % 128 == 0 else pltpu.roll(value, (-by) % 128, 1)


def main_kernel(
    got_ref, ahead_ref, forward_ref, backward_ref, fields_ref, class_ref, back_hbm,
    margin_ref, grad_ref,
    turned_ref, minus_ref, key_ref, att_ref, turn_ref, pg_ref, place_ref, live_ref,
    lift_ref, slope_ref, act_first, act_ref, act_back, mix_ref, mix_next, mix_back, back_ref, sum_ref, count_ref, back_sem,
):
    total = got_ref.shape[0] * ROWS
    back_copy = pltpu.make_async_copy(back_hbm, turned_ref, back_sem)
    back_copy.start()
    got = got_ref[...].reshape(total, 128)
    picker = (iota((8, 128), 1) == INFO + iota((8, 128), 0)).astype(BF16)
    facts = dot(picker, got, NT)
    spot = iota((1, total), 1)
    within = spot % ROWS
    is_slot = (within < 8) & (within % 2 == 1)
    me = facts[6:7]
    mine = is_slot & (facts[2:3] > 0.5) & (facts[0:1] == me)
    here = is_slot & ((spot // ROWS).astype(F32) == me)
    marks = jnp.broadcast_to(mine.astype(F32), (8, total))
    before = (iota((128, 128), 0) < iota((128, 128), 1)).astype(BF16)
    carry, ranks = jnp.zeros((8, 1), F32), []
    for block in range(total // 128):
        part = marks[:, block * 128 : block * 128 + 128]
        ranks.append(dot(part.astype(BF16), before, NN) + carry)
        carry = carry + jnp.sum(part, axis=1, keepdims=True)
    ranks = jnp.concatenate(ranks, axis=1)
    owned = carry[0:1]
    key_mine = jnp.where(mine, ranks[0:1], -1.0)
    key_here = jnp.where(here, (within // 2).astype(F32) + 2.0 * jnp.floor((owned + 1.0) * 0.5), -1.0)
    key_ref[...] = jnp.concatenate([key_mine, key_here, jnp.full((6, total), -1.0, F32)], axis=0)
    pairs = (jnp.sum(owned).astype(jnp.int32) + 1) // 2

    for tap in range(9):
        for f in (1, 2, 3):
            minus_ref[tap, f - 1] = -ahead_ref[tap, 2 * f + 1]
    sum_ref[...] = jnp.zeros_like(sum_ref)
    count_ref[...] = jnp.zeros_like(count_ref)
    for ref in (act_first, act_ref, act_back):
        ref[:, 0:16, :] = jnp.zeros((3, 16, 1024), BF16)
        ref[:, 144:160, :] = jnp.zeros((3, 16, 1024), BF16)

    def gather(first_pair):
        height = GROUP * 4
        lane = iota((height, 128), 1)
        odd = iota((height, 128), 0) % 8 >= 4
        colour = iota((height, 128), 0) % 4
        item = (2 * first_pair + 2 * (iota((height, 1), 0) // 8) + (iota((height, 1), 0) % 8) // 4).astype(F32)
        keys = key_ref[...]
        earlier = pltpu.roll(keys, total - 1, 1)
        second = ((keys[0:1] == item) | (keys[1:2] == item)).astype(BF16)
        first = ((earlier[0:1] == item) | (earlier[1:2] == item)).astype(BF16)
        rows2 = dot(second, got, NN)
        rows1 = dot(first, got, NN)
        owner, step, live, label, half = [rows2[:, INFO + i : INFO + i + 1] for i in (0, 1, 2, 3, 5)]
        owns = item < owned
        source = jnp.where(owns, float(total) + step, owner * float(ROWS) + step + 8.0)
        again = jnp.where(owns, source + 12.0, -1.0)
        number = iota((1, total + 128), 1).astype(F32)
        picks = ((number == source) | (number == again)).astype(BF16)
        angle = dot(picks[:, 0:total], got, NN) + dot(picks[:, total:], fields_ref[...], NN)
        angle = jnp.where((half > 0.5) == odd, angle, pltpu.roll(angle, PIX, 1))
        turned1, turned2 = pltpu.roll(rows1, PIX, 1), pltpu.roll(rows2, PIX, 1)
        red = jnp.where(odd, turned1, rows1)
        green = jnp.where(odd, rows1, turned1)
        blue = jnp.where(odd, turned2, rows2)
        own = jnp.where(colour == 0, red, jnp.where(colour == 1, green, blue))
        cross = SKEW * jnp.where(colour == 0, blue - green, jnp.where(colour == 1, red - blue, green - red))
        grey = (red + green + blue) * (1.0 / 3.0)
        sin, cos = sin_cos(angle, angle * angle)
        valid = (colour < 3) & ((lane >= PIX) == odd)
        shade = own - grey
        attacked = jnp.where(valid, grey + cos * shade + sin * cross, 0.0).reshape(GROUP // 2, 8, 128)
        turning = jnp.where(valid, cos * cross - sin * shade, 0.0).reshape(GROUP // 2, 8, 128)
        classes = class_ref.shape[0]
        score = jnp.where(lane < classes, PIX * (1.0 / classes - (lane.astype(F32) == label).astype(F32)), 0.0)
        gain = dot(score[:, 0:classes], class_ref[...], NN, lax.Precision.HIGHEST)
        place = jnp.where(owns, 2.0 * step + half, -1.0)
        spots = pl.ds(first_pair, GROUP // 2)
        att_ref[spots] = attacked + pltpu.roll(attacked, 4, 1)
        turn_ref[spots] = turning + pltpu.roll(turning, 4, 1)
        pg_ref[spots] = gain.reshape(GROUP // 2, 8, 128)
        place_ref[spots] = jnp.broadcast_to(place, (height, 128)).reshape(GROUP // 2, 8, 128)
        live_ref[spots] = jnp.broadcast_to(live, (height, 128)).reshape(GROUP // 2, 8, 128)

    inner_less = jnp.where(iota((16, 128), 0) % 8 == 0, 0.0, 1.0).astype(BF16)
    inner_more = jnp.where(iota((16, 128), 0) % 8 == 7, 0.0, 1.0).astype(BF16)

    def put(act, y, number, value):
        turns = value.reshape(2, 8, 128)
        less = pltpu.roll(turns, 1, 1).reshape(16, 128).astype(BF16) * inner_less
        more = pltpu.roll(turns, 7, 1).reshape(16, 128).astype(BF16) * inner_more
        for which, part in enumerate((less, value.astype(BF16), more)):
            act[which, 16 * y + 16 : 16 * y + 32, 128 * number : 128 * number + 128] = part

    def lift(pair, act, slope):
        def start():
            value = att_ref[pair]
            upper = value.astype(BF16).astype(F32)
            value = jnp.where(iota((8, 128), 0) < 4, upper, value - upper)
            taps = [
                jnp.where(tap_mask(tap // 3 - 1, tap % 3 - 1), shifted(value, 8 * (tap // 3 - 1) + tap % 3 - 1), 0.0)
                for tap in range(9)
            ]
            patches = jnp.concatenate(taps + taps, axis=0).astype(BF16)
            lift_ref[...] = dot(patches, forward_ref[...], TN).reshape(2, 8, 8, 384)

        def line(y):
            lifted = lift_ref[:, y].reshape(16, 384)
            g, p, q = lifted[:, 0:128], lifted[:, 128:256], lifted[:, 256:384]
            minus, plus = (p - q) * HALF, (p + q) * HALF
            hues = [g + p, g + minus, g - q, g - plus, g - p, g - minus, g + q, g + plus]
            activated = []
            for k, h in enumerate(hues):
                t = jnp.tanh(h)
                one = 1.0 + t
                value = h * one
                slope_ref[slope, 16 * y : 16 * y + 16, 128 * k : 128 * k + 128] = one + value * (1.0 - t)
                activated.append(value)
            for number, part in enumerate(hue_fourier(activated)):
                put(act, y, number, part)

        return [start] + [functools.partial(line, y) for y in range(8)]

    def convolve(act, out, forward):
        def moved(tap, columns):
            dy, dx = (tap // 3, tap % 3) if forward else (2 - tap // 3, 2 - tap % 3)
            return act[dx, 16 * dy : 16 * dy + 128, columns]

        weights = ahead_ref if forward else turned_ref

        def part(f):
            columns = slice(256 * f, 256 * f + 256)
            right = []
            for tap in range(9):
                if f == 0:
                    zero = jnp.zeros((128, 128), BF16)
                    square = ((weights[tap, 0], zero), (zero, weights[tap, 1]))
                elif forward:
                    re, im, minus = weights[tap, 2 * f], weights[tap, 2 * f + 1], minus_ref[tap, f - 1]
                    square = ((re, minus), (im, re))
                else:
                    re, minus, im = [weights[tap, 3 * f - 1 + i] for i in range(3)]
                    square = ((re, im), (minus, re))
                right += [jnp.concatenate(pieces, axis=1) for pieces in square]
            left = jnp.concatenate([moved(tap, columns) for tap in range(9)], axis=1)
            out[:, columns] = dot(left, jnp.concatenate(right, axis=0), NN)

        return [functools.partial(part, f) for f in range(4)]

    def gains(pair):
        return [pg_ref[pair][4 * t : 4 * t + 1] for t in range(2)]

    def slopes(pair, mix):
        spread = jnp.concatenate([jnp.broadcast_to(g, (8, 128)) for g in gains(pair)], axis=0) * (0.5 / 512.0)

        def line(y):
            parts = [mix[16 * y : 16 * y + 16, 128 * k : 128 * k + 128] for k in range(8)]
            slope = []
            for h in hue_inverse(parts):
                t = jnp.tanh(h)
                one = 1.0 + t
                slope.append((one + (h * one) * (1.0 - t)) * spread)
            for number, part in enumerate(hue_fourier(slope)):
                put(act_back, y, number, part)

        return [functools.partial(line, y) for y in range(8)]

    def pool(pair, mix):
        sums = []

        def line(y):
            parts = [mix[16 * y : 16 * y + 16, 128 * k : 128 * k + 128] for k in range(8)]
            values = [h * (1.0 + jnp.tanh(h)) for h in hue_inverse(parts)]
            while len(values) > 1:
                values = [a + b for a, b in zip(values[::2], values[1::2])]
            sums[:] = [sums[0] + values[0]] if sums else values

        def finish():
            pooled = jnp.sum(sums[0].reshape(2, 8, 128), axis=1)
            gain = jnp.concatenate(gains(pair), axis=0)
            margin = jnp.sum(pooled * gain, axis=1, keepdims=True) * (-1.0 / (PIX * 512.0))
            live = live_ref[pair]
            return [margin[t : t + 1] * live[4 * t : 4 * t + 1] for t in range(2)]

        return [functools.partial(line, y) for y in range(8)], finish

    def back(pair, slope, wanted):
        def line(y):
            parts = [mix_back[16 * y : 16 * y + 16, 128 * k : 128 * k + 128] for k in range(8)]
            grads = [
                part * slope_ref[slope, 16 * y : 16 * y + 16, 128 * k : 128 * k + 128]
                for k, part in enumerate(hue_inverse(parts))
            ]
            s = [grads[i] + grads[i + 4] for i in range(4)]
            d = [grads[i] - grads[i + 4] for i in range(4)]
            minus, plus = (d[1] - d[3]) * HALF, (d[1] + d[3]) * HALF
            for i, value in enumerate(((s[0] + s[2]) + (s[1] + s[3]), d[0] + minus, -d[2] - plus)):
                upper = value.astype(BF16).astype(F32)
                for place, part in ((i, upper), (i + 3, value - upper), (i + 6, upper)):
                    back_ref[:, y, :, 128 * place : 128 * place + 128] = part.reshape(2, 8, 128)

        def finish():
            gradient = dot(backward_ref[...], back_ref[...].reshape(128, 1152).astype(BF16), NT)
            number_of = (2 * iota((16, 128), 0) + iota((16, 128), 1) // PIX).astype(F32)
            colour_grad = jnp.zeros((8, 128), F32)
            for tap in range(9):
                dy, dx = tap // 3 - 1, tap % 3 - 1
                part = gradient[8 * tap : 8 * tap + 8]
                colour_grad += jnp.where(tap_mask(-dy, -dx), shifted(part, -8 * dy - dx), 0.0)
            angle_grad = jnp.sum(colour_grad * turn_ref[pair], axis=0, keepdims=True)
            turned = pltpu.roll(jnp.broadcast_to(angle_grad, (8, 128)), PIX, 1)[0:1]
            places = jnp.where(wanted, place_ref[pair], -1.0)
            for t in range(2):
                chosen = jnp.where((iota((1, 128), 1) >= PIX) == (t == 1), angle_grad, turned)
                same = number_of == places[4 * t : 4 * t + 1]
                sum_ref[...] += jnp.where(same, chosen, 0.0)
                count_ref[...] += same.astype(F32)

        return [functools.partial(line, y) for y in range(8)] + [finish]

    def together(*lists):
        longest = max(len(steps) for steps in lists)
        for place in range(longest):
            for steps in lists:
                for number in range(len(steps) * place // longest, len(steps) * (place + 1) // longest):
                    steps[number]()

    gather(0)
    together(lift(0, act_first, 0))
    together(convolve(act_first, mix_ref, True), lift(1, act_ref, 1))
    back_copy.wait()

    def copy_mix(y):
        mix_ref[16 * y : 16 * y + 16] = mix_next[16 * y : 16 * y + 16]

    def step(pair, _):
        after = pair + 2

        @pl.when((after % (GROUP // 2) == 0) & (after < pairs + 2))
        def _():
            gather(after)

        earlier = jnp.maximum(pair - 1, 0)
        together(
            convolve(act_ref, mix_next, True),
            slopes(pair, mix_ref),
            back(earlier, earlier % 4, pair > 0),
        )
        together(
            convolve(act_back, mix_back, False),
            lift(after, act_ref, after % 4),
            [functools.partial(copy_mix, y) for y in range(8)],
        )
        return 0

    lax.fori_loop(0, pairs, step, 0)
    lines0, margins0 = pool(pairs, mix_ref)
    last = jnp.maximum(pairs - 1, 0)
    together(convolve(act_ref, mix_next, True), back(last, last % 4, pairs > 0), lines0)
    lines1, margins1 = pool(pairs + 1, mix_next)
    together(lines1)
    margins = margins0() + margins1()
    lane1 = iota((1, 128), 1)
    result = jnp.zeros((1, 128), F32)
    for number, margin in enumerate(margins):
        result = jnp.where(lane1 == number, margin, result)
    margin_ref[...] = result[0, 0 : margin_ref.shape[0]]
    grad_ref[...] = (sum_ref[...] / jnp.maximum(count_ref[...], 1.0))[0 : grad_ref.shape[0]]


def sin_cos(angle, square):
    sin = -1.0 / 39916800.0
    for coefficient in (1.0 / 362880.0, -1.0 / 5040.0, 1.0 / 120.0, -1.0 / 6.0, 1.0):
        sin = sin * square + coefficient
    cos = 1.0 / 479001600.0
    for coefficient in (-1.0 / 3628800.0, 1.0 / 40320.0, -1.0 / 720.0, 1.0 / 24.0, -0.5, 1.0):
        cos = cos * square + coefficient
    return sin * angle, cos


def vmem(count):
    return [pl.BlockSpec(memory_space=pltpu.VMEM) for _ in range(count)]


def in_hbm(array):
    return pltpu.with_memory_space_constraint(array, pltpu.HBM)


def shards(
    tiles, tile_slide, tile_mask, tile_label, attack_field, lift_weight, group_weight, class_weight
):
    devices = lax.axis_size("tiles")
    field = attack_field.reshape(-1, 128)
    slides = attack_field.shape[0] // PIX
    message = pl.pallas_call(
        functools.partial(pack_kernel, slides),
        out_shape=jax.ShapeDtypeStruct((devices, ROWS, 128), BF16),
        in_specs=[pl.BlockSpec(memory_space=pltpu.SMEM)] * 3 + vmem(2),
        out_specs=pl.BlockSpec(memory_space=pltpu.VMEM),
        name="pack",
    )(tile_slide, tile_mask, tile_label, tiles, field)
    got = lax.all_to_all(message, "tiles", split_axis=0, concat_axis=0, tiled=True)
    hbm = pl.BlockSpec(memory_space=pltpu.HBM)
    ahead, turned, forward, backward, fields, classes = pl.pallas_call(
        weight_kernel,
        out_shape=(
            jax.ShapeDtypeStruct((9, 8, 128, 128), BF16),
            pltpu.HBM((9, 11, 128, 128), BF16),
            jax.ShapeDtypeStruct((144, 384), BF16),
            jax.ShapeDtypeStruct((80, 1152), BF16),
            jax.ShapeDtypeStruct((128, 128), BF16),
            jax.ShapeDtypeStruct(class_weight.shape[::-1], F32),
        ),
        in_specs=[hbm] * 4,
        out_specs=(*vmem(1), hbm, *vmem(4)),
        scratch_shapes=[
            pltpu.VMEM((9, 8, 128, 128), BF16),
            pltpu.VMEM((9, 3, 128), F32),
            pltpu.VMEM(field.shape, F32),
            pltpu.VMEM((9, 11, 128, 128), BF16),
            pltpu.SemaphoreType.DMA((9,)),
            pltpu.SemaphoreType.DMA((3,)),
            pltpu.SemaphoreType.DMA((9,)),
        ],
        compiler_params=pltpu.CompilerParams(vmem_limit_bytes=16 * 2**20),
        cost_estimate=pl.CostEstimate(flops=10_000_000, bytes_accessed=9_000_000, transcendentals=0),
        name="weights",
    )(in_hbm(group_weight), in_hbm(lift_weight), in_hbm(field), in_hbm(class_weight.T))
    total = devices * ROWS
    spots = devices + SLOTS // 2 + GROUP // 2
    margins, attack_grad = pl.pallas_call(
        main_kernel,
        out_shape=(jax.ShapeDtypeStruct(tile_slide.shape, F32), jax.ShapeDtypeStruct(field.shape, F32)),
        in_specs=vmem(6) + [hbm],
        out_specs=tuple(vmem(2)),
        scratch_shapes=[
            pltpu.VMEM((9, 11, 128, 128), BF16),
            pltpu.VMEM((9, 3, 128, 128), BF16),
            pltpu.VMEM((8, total), F32),
            *[pltpu.VMEM((spots, 8, 128), F32) for _ in range(5)],
            pltpu.VMEM((2, 8, 8, 384), F32),
            pltpu.VMEM((4, 128, 1024), F32),
            *[pltpu.VMEM((3, 160, 1024), BF16) for _ in range(3)],
            *[pltpu.VMEM((128, 1024), F32) for _ in range(3)],
            pltpu.VMEM((2, 8, 8, 1152), F32),
            pltpu.VMEM((16, 128), F32),
            pltpu.VMEM((16, 128), F32),
            pltpu.SemaphoreType.DMA,
        ],
        compiler_params=pltpu.CompilerParams(vmem_limit_bytes=32 * 2**20),
        cost_estimate=pl.CostEstimate(flops=4_000_000_000, bytes_accessed=9_000_000, transcendentals=2_000_000),
        name="attack",
    )(got, ahead, forward, backward, fields, classes, in_hbm(turned))
    return (margins, attack_grad.reshape(-1))


def solution(mesh):
    return jax.shard_map(
        shards,
        mesh=mesh,
        in_specs=(
            P(None, ("groups", "tiles")),
            P(("groups", "tiles")),
            P(("groups", "tiles")),
            P(("groups", "tiles")),
            P(("groups", "tiles")),
            P(),
            P(),
            P(),
        ),
        out_specs=(P(("groups", "tiles")), P(("groups", "tiles"))),
        check_vma=False,
    )
```

```python
import functools
import math

import jax
import jax.numpy as jnp
from jax import lax
from jax.experimental import pallas as pl
from jax.experimental.pallas import tpu as pltpu
from jax.sharding import PartitionSpec as P

F32 = jnp.float32
BF16 = jnp.bfloat16
PIX = 64
ROWS = 24
INFO = 64
SLOTS = 4
GROUP = 12
SKEW = 1.0 / math.sqrt(3.0)
HALF = math.sqrt(0.5)


def iota(shape, axis):
    return lax.broadcasted_iota(jnp.int32, shape, axis)


def dot(a, b, dims, precision=None):
    return lax.dot_general(a, b, (dims, ((), ())), precision=precision, preferred_element_type=F32)


NN = ((1,), (0,))
NT = ((1,), (1,))
TN = ((0,), (0,))


def hue_fourier(x):
    s = [x[i] + x[i + 4] for i in range(4)]
    d = [x[i] - x[i + 4] for i in range(4)]
    e, o = s[0] + s[2], s[1] + s[3]
    dm, dp = (d[1] - d[3]) * HALF, (d[1] + d[3]) * HALF
    return [e + o, e - o, d[0] + dm, -d[2] - dp, s[0] - s[2], s[3] - s[1], d[0] - dm, d[2] - dp]


def hue_inverse(c):
    f0, f4, r1, i1, r2, i2, r3, i3 = c
    a, b = f0 + f4, f0 - f4
    s0, s2, s1, s3 = a + r2, a - r2, b - i2, b + i2
    d0, d2 = r1 + r3, i3 - i1
    p, q = (r1 - r3) * HALF, (i1 + i3) * HALF
    d1, d3 = p - q, -p - q
    s, d = (s0, s1, s2, s3), (d0, d1, d2, d3)
    return [s[k] + d[k] for k in range(4)] + [s[k] - d[k] for k in range(4)]


def pack_kernel(slides, slide_ref, mask_ref, label_ref, tiles_ref, field_ref, out_ref):
    lane = iota((1, 128), 1)
    left = lane < PIX
    tiles = tiles_ref[...].astype(F32)
    rows, parts = [], []
    for slot in range(4):
        part = tiles[:, 128 * (slot // 2) : 128 * (slot // 2) + 128]
        turned = pltpu.roll(part, PIX, 1)
        low, high = (part, turned) if slot % 2 == 0 else (turned, part)
        slide = slide_ref[slot]
        owner = slide // slides
        place = slide - owner * slides
        facts = [owner, place // 2, mask_ref[slot], label_ref[slot], slot, place % 2]
        info = jnp.zeros((1, 128), jnp.int32)
        for number, fact in enumerate(facts):
            info = jnp.where(lane == INFO + number, fact, info)
        rows.append(jnp.where(left, low[0:1], high[1:2]))
        rows.append(jnp.where(left, low[2:3], info.astype(F32)))
    rows = jnp.concatenate(rows, axis=0)
    rest = jnp.concatenate([field_ref[...], jnp.zeros((4, 128), F32)], axis=0)
    at = (iota((8, 128), 1) == INFO + 6) & (iota((8, 128), 0) % 2 == 1)
    for target in range(out_ref.shape[0]):
        slot_rows = jnp.where(at, float(target), rows)
        out_ref[target] = jnp.concatenate([slot_rows, rest], axis=0).astype(BF16)


def weight_kernel(
    weight_hbm, lift_hbm, field_hbm, class_hbm,
    ahead, back_hbm, forward_ref, backward_ref, fields_ref, class_ref,
    raw, lift_ref, field_ref, back, in_sem, small_sem, out_sem,
):
    def fetch(tap):
        return pltpu.make_async_copy(weight_hbm.at[:, tap], raw.at[tap], in_sem.at[tap])

    def store(tap):
        return pltpu.make_async_copy(back.at[tap], back_hbm.at[tap], out_sem.at[tap])

    small = [
        pltpu.make_async_copy(source, target, small_sem.at[number])
        for number, (source, target) in enumerate(
            ((lift_hbm, lift_ref), (field_hbm, field_ref), (class_hbm, class_ref))
        )
    ]
    for copy in small:
        copy.start()
    for tap in range(9):
        fetch(tap).start()
    for copy in small:
        copy.wait()
    field = field_ref[...]
    upper = field.astype(BF16).astype(F32)
    fields_ref[...] = jnp.concatenate([upper, field - upper, jnp.zeros((104, 128), F32)], axis=0).astype(BF16)

    both, single = [], []
    for tap in range(9):
        lift = lift_ref[tap]
        l0, l1, l2 = lift[0:1], lift[1:2], lift[2:3]
        grey = (l0 + l1 + l2) * (1.0 / 3.0)
        zero = jnp.zeros((1, 128), F32)
        columns = (
            [grey] * 3,
            [l0 - grey, l1 - grey, l2 - grey],
            [(l1 - l2) * SKEW, (l2 - l0) * SKEW, (l0 - l1) * SKEW],
        )
        both.append(jnp.concatenate([jnp.concatenate([*c, zero, *c, zero], axis=0) for c in columns], axis=1))
        single.append(jnp.concatenate([jnp.concatenate([*c, *[zero] * 5], axis=0) for c in columns], axis=1))
    both = jnp.concatenate(both, axis=0) * 0.5
    upper = both.astype(BF16).astype(F32)
    forward_ref[...] = jnp.concatenate([upper, both - upper], axis=0).astype(BF16)
    single = jnp.concatenate(single + [jnp.zeros((8, 384), F32)], axis=0)
    upper = single.astype(BF16).astype(F32)
    backward_ref[...] = jnp.concatenate([upper, upper, single - upper], axis=1).astype(BF16)

    def work(tap, _):
        fetch(tap).wait()
        for block in range(0, 128, 32):
            rows = slice(block, block + 32)
            f0, f4, r1, i1, r2, i2, r3, i3 = hue_fourier([raw[tap, k, rows, :].astype(F32) for k in range(8)])
            parts = [f0 * 0.0625, f4 * 0.0625] + [part * 0.125 for part in (r1, i1, r2, i2, r3, i3)]
            for number, part in enumerate(parts):
                ahead[tap, number, rows, :] = part.astype(BF16)
        for number in (0, 1):
            back[tap, number] = ahead[tap, number].T
        for f in (1, 2, 3):
            back[tap, 3 * f - 1] = ahead[tap, 2 * f].T
            im = ahead[tap, 2 * f + 1].T
            back[tap, 3 * f] = -im
            back[tap, 3 * f + 1] = im
        store(tap).start()
        return 0

    lax.fori_loop(0, 9, work, 0)
    for tap in range(9):
        store(tap).wait()


def tap_mask(dy, dx):
    lane = iota((1, 128), 1)
    x, y = lane % 8 + dx, (lane // 8) % 8 + dy
    return (x >= 0) & (x < 8) & (y >= 0) & (y < 8)


def shifted(value, by):
    return value if by % 128 == 0 else pltpu.roll(value, (-by) % 128, 1)


def main_kernel(
    got_ref, ahead_ref, forward_ref, backward_ref, fields_ref, class_ref, back_hbm,
    margin_ref, grad_ref,
    turned_ref, minus_ref, key_ref, att_ref, turn_ref, pg_ref, place_ref, slot_ref,
    lift_ref, slope_ref, act_first, act_ref, act_back, mix_ref, mix_next, mix_back, back_ref, sum_ref, count_ref, pool_ref, back_sem,
):
    total = got_ref.shape[0] * ROWS
    back_copy = pltpu.make_async_copy(back_hbm, turned_ref, back_sem)
    back_copy.start()
    got = got_ref[...].reshape(total, 128)
    picker = (iota((8, 128), 1) == INFO + iota((8, 128), 0)).astype(BF16)
    facts = dot(picker, got, NT)
    spot = iota((1, total), 1)
    within = spot % ROWS
    is_slot = (within < 8) & (within % 2 == 1)
    me = facts[6:7]
    live = is_slot & (facts[2:3] > 0.5)
    mine = live & (facts[0:1] == me)
    here = live & ((spot // ROWS).astype(F32) == me)
    marks = jnp.concatenate([mine.astype(F32), here.astype(F32), jnp.zeros((6, total), F32)], axis=0)
    before = (iota((128, 128), 0) < iota((128, 128), 1)).astype(BF16)
    carry, ranks = jnp.zeros((8, 1), F32), []
    for block in range(total // 128):
        part = marks[:, block * 128 : block * 128 + 128]
        ranks.append(dot(part.astype(BF16), before, NN) + carry)
        carry = carry + jnp.sum(part, axis=1, keepdims=True)
    ranks = jnp.concatenate(ranks, axis=1)
    owned, slots = carry[0:1], carry[1:2]
    key_mine = jnp.where(mine, ranks[0:1], -1.0)
    key_here = jnp.where(here, ranks[1:2] + owned, -1.0)
    key_ref[...] = jnp.concatenate([key_mine, key_here, jnp.full((6, total), -1.0, F32)], axis=0)
    owned_count = jnp.sum(owned).astype(jnp.int32)
    pairs = (owned_count + 1) // 2
    all_pairs = (owned_count + jnp.sum(slots).astype(jnp.int32) + 1) // 2

    for tap in range(9):
        for f in (1, 2, 3):
            minus_ref[tap, f - 1] = -ahead_ref[tap, 2 * f + 1]
    sum_ref[...] = jnp.zeros_like(sum_ref)
    count_ref[...] = jnp.zeros_like(count_ref)
    for ref in (act_first, act_ref, act_back):
        ref[:, 0:16, :] = jnp.zeros((3, 16, 1024), BF16)
        ref[:, 144:160, :] = jnp.zeros((3, 16, 1024), BF16)

    def gather(first_pair):
        height = GROUP * 4
        lane = iota((height, 128), 1)
        odd = iota((height, 128), 0) % 8 >= 4
        colour = iota((height, 128), 0) % 4
        item = (2 * first_pair + 2 * (iota((height, 1), 0) // 8) + (iota((height, 1), 0) % 8) // 4).astype(F32)
        keys = key_ref[...]
        earlier = pltpu.roll(keys, total - 1, 1)
        second = ((keys[0:1] == item) | (keys[1:2] == item)).astype(BF16)
        first = ((earlier[0:1] == item) | (earlier[1:2] == item)).astype(BF16)
        rows2 = dot(second, got, NN)
        rows1 = dot(first, got, NN)
        owner, step, label, slot, half = [rows2[:, INFO + i : INFO + i + 1] for i in (0, 1, 3, 4, 5)]
        owns = item < owned
        source = jnp.where(owns, float(total) + step, owner * float(ROWS) + step + 8.0)
        again = jnp.where(owns, source + 12.0, -1.0)
        number = iota((1, total + 128), 1).astype(F32)
        picks = ((number == source) | (number == again)).astype(BF16)
        angle = dot(picks[:, 0:total], got, NN) + dot(picks[:, total:], fields_ref[...], NN)
        angle = jnp.where((half > 0.5) == odd, angle, pltpu.roll(angle, PIX, 1))
        turned1, turned2 = pltpu.roll(rows1, PIX, 1), pltpu.roll(rows2, PIX, 1)
        red = jnp.where(odd, turned1, rows1)
        green = jnp.where(odd, rows1, turned1)
        blue = jnp.where(odd, turned2, rows2)
        own = jnp.where(colour == 0, red, jnp.where(colour == 1, green, blue))
        cross = SKEW * jnp.where(colour == 0, blue - green, jnp.where(colour == 1, red - blue, green - red))
        grey = (red + green + blue) * (1.0 / 3.0)
        sin, cos = sin_cos(angle, angle * angle)
        valid = (colour < 3) & ((lane >= PIX) == odd)
        shade = own - grey
        attacked = jnp.where(valid, grey + cos * shade + sin * cross, 0.0).reshape(GROUP // 2, 8, 128)
        turning = jnp.where(valid, cos * cross - sin * shade, 0.0).reshape(GROUP // 2, 8, 128)
        classes = class_ref.shape[0]
        score = jnp.where(lane < classes, PIX * (1.0 / classes - (lane.astype(F32) == label).astype(F32)), 0.0)
        gain = dot(score[:, 0:classes], class_ref[...], NN, lax.Precision.HIGHEST)
        place = jnp.where(owns, 2.0 * step + half, -1.0)
        spots = pl.ds(first_pair, GROUP // 2)
        att_ref[spots] = attacked + pltpu.roll(attacked, 4, 1)
        turn_ref[spots] = turning + pltpu.roll(turning, 4, 1)
        pg_ref[spots] = gain.reshape(GROUP // 2, 8, 128)
        place_ref[spots] = jnp.broadcast_to(place, (height, 128)).reshape(GROUP // 2, 8, 128)
        slot = jnp.where((item >= owned) & (item < owned + slots), slot, -1.0)
        slot_ref[spots] = jnp.broadcast_to(slot, (height, 128)).reshape(GROUP // 2, 8, 128)

    inner_less = jnp.where(iota((16, 128), 0) % 8 == 0, 0.0, 1.0).astype(BF16)
    inner_more = jnp.where(iota((16, 128), 0) % 8 == 7, 0.0, 1.0).astype(BF16)

    def put(act, y, number, value):
        turns = value.reshape(2, 8, 128)
        less = pltpu.roll(turns, 1, 1).reshape(16, 128).astype(BF16) * inner_less
        more = pltpu.roll(turns, 7, 1).reshape(16, 128).astype(BF16) * inner_more
        for which, part in enumerate((less, value.astype(BF16), more)):
            act[which, 16 * y + 16 : 16 * y + 32, 128 * number : 128 * number + 128] = part

    def lift(pair, act, slope):
        def start():
            value = att_ref[pair]
            upper = value.astype(BF16).astype(F32)
            value = jnp.where(iota((8, 128), 0) < 4, upper, value - upper)
            taps = [
                jnp.where(tap_mask(tap // 3 - 1, tap % 3 - 1), shifted(value, 8 * (tap // 3 - 1) + tap % 3 - 1), 0.0)
                for tap in range(9)
            ]
            patches = jnp.concatenate(taps + taps, axis=0).astype(BF16)
            lift_ref[...] = dot(patches, forward_ref[...], TN).reshape(2, 8, 8, 384)

        def line(y):
            lifted = lift_ref[:, y].reshape(16, 384)
            g, p, q = lifted[:, 0:128], lifted[:, 128:256], lifted[:, 256:384]
            minus, plus = (p - q) * HALF, (p + q) * HALF
            hues = [g + p, g + minus, g - q, g - plus, g - p, g - minus, g + q, g + plus]
            activated = []
            for k, h in enumerate(hues):
                t = jnp.tanh(h)
                one = 1.0 + t
                value = h * one
                slope_ref[slope, 16 * y : 16 * y + 16, 128 * k : 128 * k + 128] = one + value * (1.0 - t)
                activated.append(value)
            for number, part in enumerate(hue_fourier(activated)):
                put(act, y, number, part)

        return [start] + [functools.partial(line, y) for y in range(8)]

    def convolve(act, out, forward):
        def moved(tap, columns):
            dy, dx = (tap // 3, tap % 3) if forward else (2 - tap // 3, 2 - tap % 3)
            return act[dx, 16 * dy : 16 * dy + 128, columns]

        weights = ahead_ref if forward else turned_ref

        def part(f):
            columns = slice(256 * f, 256 * f + 256)
            right = []
            for tap in range(9):
                if f == 0:
                    zero = jnp.zeros((128, 128), BF16)
                    square = ((weights[tap, 0], zero), (zero, weights[tap, 1]))
                elif forward:
                    re, im, minus = weights[tap, 2 * f], weights[tap, 2 * f + 1], minus_ref[tap, f - 1]
                    square = ((re, minus), (im, re))
                else:
                    re, minus, im = [weights[tap, 3 * f - 1 + i] for i in range(3)]
                    square = ((re, im), (minus, re))
                right += [jnp.concatenate(pieces, axis=1) for pieces in square]
            left = jnp.concatenate([moved(tap, columns) for tap in range(9)], axis=1)
            out[:, columns] = dot(left, jnp.concatenate(right, axis=0), NN)

        return [functools.partial(part, f) for f in range(4)]

    def gains(pair):
        return [pg_ref[pair][4 * t : 4 * t + 1] for t in range(2)]

    def add_up(pair, y, values):
        while len(values) > 1:
            values = [a + b for a, b in zip(values[::2], values[1::2])]
        pool_ref[pair] = values[0] if y == 0 else pool_ref[pair] + values[0]

    def slopes(pair, mix):
        spread = jnp.concatenate([jnp.broadcast_to(g, (8, 128)) for g in gains(pair)], axis=0) * (0.5 / 512.0)

        def line(y):
            parts = [mix[16 * y : 16 * y + 16, 128 * k : 128 * k + 128] for k in range(8)]
            slope, values = [], []
            for h in hue_inverse(parts):
                t = jnp.tanh(h)
                one = 1.0 + t
                value = h * one
                values.append(value)
                slope.append((one + value * (1.0 - t)) * spread)
            add_up(pair, y, values)
            for number, part in enumerate(hue_fourier(slope)):
                put(act_back, y, number, part)

        return [functools.partial(line, y) for y in range(8)]

    def pool(pair, mix):
        def line(y):
            parts = [mix[16 * y : 16 * y + 16, 128 * k : 128 * k + 128] for k in range(8)]
            add_up(pair, y, [h * (1.0 + jnp.tanh(h)) for h in hue_inverse(parts)])

        return [functools.partial(line, y) for y in range(8)]

    def margins(pair, wanted):
        pooled = jnp.sum(pool_ref[pair].reshape(2, 8, 128), axis=1)
        gain = jnp.concatenate(gains(pair), axis=0)
        margin = jnp.sum(pooled * gain, axis=1, keepdims=True) * (-1.0 / (PIX * 512.0))
        at = jnp.where(wanted, slot_ref[pair], -1.0)
        lanes = iota((1, 128), 1).astype(F32)
        return sum(jnp.where(lanes == at[4 * t : 4 * t + 1], margin[t : t + 1], 0.0) for t in range(2))

    def back(pair, slope, wanted):
        def line(y):
            parts = [mix_back[16 * y : 16 * y + 16, 128 * k : 128 * k + 128] for k in range(8)]
            grads = [
                part * slope_ref[slope, 16 * y : 16 * y + 16, 128 * k : 128 * k + 128]
                for k, part in enumerate(hue_inverse(parts))
            ]
            s = [grads[i] + grads[i + 4] for i in range(4)]
            d = [grads[i] - grads[i + 4] for i in range(4)]
            minus, plus = (d[1] - d[3]) * HALF, (d[1] + d[3]) * HALF
            for i, value in enumerate(((s[0] + s[2]) + (s[1] + s[3]), d[0] + minus, -d[2] - plus)):
                upper = value.astype(BF16).astype(F32)
                for place, part in ((i, upper), (i + 3, value - upper), (i + 6, upper)):
                    back_ref[:, y, :, 128 * place : 128 * place + 128] = part.reshape(2, 8, 128)

        def finish():
            gradient = dot(backward_ref[...], back_ref[...].reshape(128, 1152).astype(BF16), NT)
            number_of = (2 * iota((16, 128), 0) + iota((16, 128), 1) // PIX).astype(F32)
            colour_grad = jnp.zeros((8, 128), F32)
            for tap in range(9):
                dy, dx = tap // 3 - 1, tap % 3 - 1
                part = gradient[8 * tap : 8 * tap + 8]
                colour_grad += jnp.where(tap_mask(-dy, -dx), shifted(part, -8 * dy - dx), 0.0)
            angle_grad = jnp.sum(colour_grad * turn_ref[pair], axis=0, keepdims=True)
            turned = pltpu.roll(jnp.broadcast_to(angle_grad, (8, 128)), PIX, 1)[0:1]
            places = jnp.where(wanted, place_ref[pair], -1.0)
            for t in range(2):
                chosen = jnp.where((iota((1, 128), 1) >= PIX) == (t == 1), angle_grad, turned)
                same = number_of == places[4 * t : 4 * t + 1]
                sum_ref[...] += jnp.where(same, chosen, 0.0)
                count_ref[...] += same.astype(F32)

        return [functools.partial(line, y) for y in range(8)] + [finish]

    def together(*lists):
        longest = max(len(steps) for steps in lists)
        for place in range(longest):
            for steps in lists:
                for number in range(len(steps) * place // longest, len(steps) * (place + 1) // longest):
                    steps[number]()

    gather(0)
    together(lift(0, act_first, 0))
    together(convolve(act_first, mix_ref, True), lift(1, act_ref, 1))
    back_copy.wait()

    def copy_mix(y):
        mix_ref[16 * y : 16 * y + 16] = mix_next[16 * y : 16 * y + 16]

    def step(pair, _):
        after = pair + 2

        @pl.when((after % (GROUP // 2) == 0) & (after < pairs + 2))
        def _():
            gather(after)

        earlier = jnp.maximum(pair - 1, 0)
        together(
            convolve(act_ref, mix_next, True),
            slopes(pair, mix_ref),
            back(earlier, earlier % 4, pair > 0),
        )
        together(
            convolve(act_back, mix_back, False),
            lift(after, act_ref, after % 4),
            [functools.partial(copy_mix, y) for y in range(8)],
        )
        return 0

    lax.fori_loop(0, pairs, step, 0)
    last = jnp.maximum(pairs - 1, 0)

    @pl.when(all_pairs - pairs > 1)
    def _():
        together(
            convolve(act_ref, mix_next, True), back(last, last % 4, pairs > 0), pool(pairs, mix_ref)
        )
        together(pool(pairs + 1, mix_next))

    @pl.when(all_pairs - pairs <= 1)
    def _():
        together(back(last, last % 4, pairs > 0), pool(pairs, mix_ref))

    result = margins(last, pairs > 0) + margins(pairs, all_pairs > pairs) + margins(pairs + 1, all_pairs > pairs + 1)
    margin_ref[...] = result[0, 0 : margin_ref.shape[0]]
    grad_ref[...] = (sum_ref[...] / jnp.maximum(count_ref[...], 1.0))[0 : grad_ref.shape[0]]


def sin_cos(angle, square):
    sin = -1.0 / 39916800.0
    for coefficient in (1.0 / 362880.0, -1.0 / 5040.0, 1.0 / 120.0, -1.0 / 6.0, 1.0):
        sin = sin * square + coefficient
    cos = 1.0 / 479001600.0
    for coefficient in (-1.0 / 3628800.0, 1.0 / 40320.0, -1.0 / 720.0, 1.0 / 24.0, -0.5, 1.0):
        cos = cos * square + coefficient
    return sin * angle, cos


def vmem(count):
    return [pl.BlockSpec(memory_space=pltpu.VMEM) for _ in range(count)]


def in_hbm(array):
    return pltpu.with_memory_space_constraint(array, pltpu.HBM)


def shards(
    tiles, tile_slide, tile_mask, tile_label, attack_field, lift_weight, group_weight, class_weight
):
    devices = lax.axis_size("tiles")
    field = attack_field.reshape(-1, 128)
    slides = attack_field.shape[0] // PIX
    message = pl.pallas_call(
        functools.partial(pack_kernel, slides),
        out_shape=jax.ShapeDtypeStruct((devices, ROWS, 128), BF16),
        in_specs=[pl.BlockSpec(memory_space=pltpu.SMEM)] * 3 + vmem(2),
        out_specs=pl.BlockSpec(memory_space=pltpu.VMEM),
        name="pack",
    )(tile_slide, tile_mask, tile_label, tiles, field)
    got = lax.all_to_all(message, "tiles", split_axis=0, concat_axis=0, tiled=True)
    hbm = pl.BlockSpec(memory_space=pltpu.HBM)
    ahead, turned, forward, backward, fields, classes = pl.pallas_call(
        weight_kernel,
        out_shape=(
            jax.ShapeDtypeStruct((9, 8, 128, 128), BF16),
            pltpu.HBM((9, 11, 128, 128), BF16),
            jax.ShapeDtypeStruct((144, 384), BF16),
            jax.ShapeDtypeStruct((80, 1152), BF16),
            jax.ShapeDtypeStruct((128, 128), BF16),
            jax.ShapeDtypeStruct(class_weight.shape[::-1], F32),
        ),
        in_specs=[hbm] * 4,
        out_specs=(*vmem(1), hbm, *vmem(4)),
        scratch_shapes=[
            pltpu.VMEM((9, 8, 128, 128), BF16),
            pltpu.VMEM((9, 3, 128), F32),
            pltpu.VMEM(field.shape, F32),
            pltpu.VMEM((9, 11, 128, 128), BF16),
            pltpu.SemaphoreType.DMA((9,)),
            pltpu.SemaphoreType.DMA((3,)),
            pltpu.SemaphoreType.DMA((9,)),
        ],
        compiler_params=pltpu.CompilerParams(vmem_limit_bytes=16 * 2**20),
        cost_estimate=pl.CostEstimate(flops=10_000_000, bytes_accessed=9_000_000, transcendentals=0),
        name="weights",
    )(in_hbm(group_weight), in_hbm(lift_weight), in_hbm(field), in_hbm(class_weight.T))
    total = devices * ROWS
    spots = devices + SLOTS // 2 + GROUP // 2
    margins, attack_grad = pl.pallas_call(
        main_kernel,
        out_shape=(jax.ShapeDtypeStruct(tile_slide.shape, F32), jax.ShapeDtypeStruct(field.shape, F32)),
        in_specs=vmem(6) + [hbm],
        out_specs=tuple(vmem(2)),
        scratch_shapes=[
            pltpu.VMEM((9, 11, 128, 128), BF16),
            pltpu.VMEM((9, 3, 128, 128), BF16),
            pltpu.VMEM((8, total), F32),
            *[pltpu.VMEM((spots, 8, 128), F32) for _ in range(5)],
            pltpu.VMEM((2, 8, 8, 384), F32),
            pltpu.VMEM((4, 128, 1024), F32),
            *[pltpu.VMEM((3, 160, 1024), BF16) for _ in range(3)],
            *[pltpu.VMEM((128, 1024), F32) for _ in range(3)],
            pltpu.VMEM((2, 8, 8, 1152), F32),
            pltpu.VMEM((16, 128), F32),
            pltpu.VMEM((16, 128), F32),
            pltpu.VMEM((spots, 16, 128), F32),
            pltpu.SemaphoreType.DMA,
        ],
        compiler_params=pltpu.CompilerParams(vmem_limit_bytes=32 * 2**20),
        cost_estimate=pl.CostEstimate(flops=4_000_000_000, bytes_accessed=9_000_000, transcendentals=2_000_000),
        name="attack",
    )(got, ahead, forward, backward, fields, classes, in_hbm(turned))
    return (margins, attack_grad.reshape(-1))


def solution(mesh):
    return jax.shard_map(
        shards,
        mesh=mesh,
        in_specs=(
            P(None, ("groups", "tiles")),
            P(("groups", "tiles")),
            P(("groups", "tiles")),
            P(("groups", "tiles")),
            P(("groups", "tiles")),
            P(),
            P(),
            P(),
        ),
        out_specs=(P(("groups", "tiles")), P(("groups", "tiles"))),
        check_vma=False,
    )
```

```python
import functools
import math

import jax
import jax.numpy as jnp
from jax import lax
from jax.experimental import pallas as pl
from jax.experimental.pallas import tpu as pltpu
from jax.sharding import PartitionSpec as P

F32 = jnp.float32
BF16 = jnp.bfloat16
PIX = 64
ROWS = 24
INFO = 64
SLOTS = 4
GROUP = 12
SKEW = 1.0 / math.sqrt(3.0)
HALF = math.sqrt(0.5)


def iota(shape, axis):
    return lax.broadcasted_iota(jnp.int32, shape, axis)


def dot(a, b, dims, precision=None):
    return lax.dot_general(a, b, (dims, ((), ())), precision=precision, preferred_element_type=F32)


NN = ((1,), (0,))
NT = ((1,), (1,))
TN = ((0,), (0,))


def hue_fourier(x):
    s = [x[i] + x[i + 4] for i in range(4)]
    d = [x[i] - x[i + 4] for i in range(4)]
    e, o = s[0] + s[2], s[1] + s[3]
    dm, dp = (d[1] - d[3]) * HALF, (d[1] + d[3]) * HALF
    return [e + o, e - o, d[0] + dm, -d[2] - dp, s[0] - s[2], s[3] - s[1], d[0] - dm, d[2] - dp]


def hue_inverse(c):
    f0, f4, r1, i1, r2, i2, r3, i3 = c
    a, b = f0 + f4, f0 - f4
    s0, s2, s1, s3 = a + r2, a - r2, b - i2, b + i2
    d0, d2 = r1 + r3, i3 - i1
    p, q = (r1 - r3) * HALF, (i1 + i3) * HALF
    d1, d3 = p - q, -p - q
    s, d = (s0, s1, s2, s3), (d0, d1, d2, d3)
    return [s[k] + d[k] for k in range(4)] + [s[k] - d[k] for k in range(4)]


def pack_kernel(slides, slide_ref, mask_ref, label_ref, tiles_ref, field_ref, out_ref):
    lane = iota((1, 128), 1)
    left = lane < PIX
    tiles = tiles_ref[...].astype(F32)
    rows, parts = [], []
    for slot in range(4):
        part = tiles[:, 128 * (slot // 2) : 128 * (slot // 2) + 128]
        turned = pltpu.roll(part, PIX, 1)
        low, high = (part, turned) if slot % 2 == 0 else (turned, part)
        slide = slide_ref[slot]
        owner = slide // slides
        place = slide - owner * slides
        facts = [owner, place // 2, mask_ref[slot], label_ref[slot], slot, place % 2]
        info = jnp.zeros((1, 128), jnp.int32)
        for number, fact in enumerate(facts):
            info = jnp.where(lane == INFO + number, fact, info)
        rows.append(jnp.where(left, low[0:1], high[1:2]))
        rows.append(jnp.where(left, low[2:3], info.astype(F32)))
    rows = jnp.concatenate(rows, axis=0)
    rest = jnp.concatenate([field_ref[...], jnp.zeros((4, 128), F32)], axis=0)
    at = (iota((8, 128), 1) == INFO + 6) & (iota((8, 128), 0) % 2 == 1)
    for target in range(out_ref.shape[0]):
        slot_rows = jnp.where(at, float(target), rows)
        out_ref[target] = jnp.concatenate([slot_rows, rest], axis=0).astype(BF16)


def weight_kernel(
    weight_hbm, lift_hbm, field_hbm, class_hbm,
    ahead, back_hbm, forward_ref, backward_ref, fields_ref, parts_ref, mean_ref,
    raw, lift_ref, field_ref, class_ref, back, in_sem, small_sem, out_sem,
):
    def fetch(tap):
        return pltpu.make_async_copy(weight_hbm.at[:, tap], raw.at[tap], in_sem.at[tap])

    def store(tap):
        return pltpu.make_async_copy(back.at[tap], back_hbm.at[tap], out_sem.at[tap])

    small = [
        pltpu.make_async_copy(source, target, small_sem.at[number])
        for number, (source, target) in enumerate(
            ((lift_hbm, lift_ref), (field_hbm, field_ref), (class_hbm, class_ref))
        )
    ]
    for copy in small:
        copy.start()
    for tap in range(9):
        fetch(tap).start()
    for copy in small:
        copy.wait()
    field = field_ref[...]
    upper = field.astype(BF16).astype(F32)
    fields_ref[...] = jnp.concatenate([upper, field - upper, jnp.zeros((104, 128), F32)], axis=0).astype(BF16)
    weight = class_ref[...]
    upper = weight.astype(BF16).astype(F32)
    middle = (weight - upper).astype(BF16).astype(F32)
    empty = jnp.zeros((128 - 3 * weight.shape[0], 128), F32)
    parts_ref[...] = jnp.concatenate([upper, middle, weight - upper - middle, empty], axis=0).astype(BF16)
    mean_ref[...] = jnp.mean(weight, axis=0, keepdims=True)

    both, single = [], []
    for tap in range(9):
        lift = lift_ref[tap]
        l0, l1, l2 = lift[0:1], lift[1:2], lift[2:3]
        grey = (l0 + l1 + l2) * (1.0 / 3.0)
        zero = jnp.zeros((1, 128), F32)
        columns = (
            [grey] * 3,
            [l0 - grey, l1 - grey, l2 - grey],
            [(l1 - l2) * SKEW, (l2 - l0) * SKEW, (l0 - l1) * SKEW],
        )
        both.append(jnp.concatenate([jnp.concatenate([*c, zero, *c, zero], axis=0) for c in columns], axis=1))
        single.append(jnp.concatenate([jnp.concatenate([*c, *[zero] * 5], axis=0) for c in columns], axis=1))
    both = jnp.concatenate(both, axis=0) * 0.5
    upper = both.astype(BF16).astype(F32)
    forward_ref[...] = jnp.concatenate([upper, both - upper], axis=0).astype(BF16)
    single = jnp.concatenate(single + [jnp.zeros((8, 384), F32)], axis=0)
    upper = single.astype(BF16).astype(F32)
    backward_ref[...] = jnp.concatenate([upper, upper, single - upper], axis=1).astype(BF16)

    def work(tap, _):
        fetch(tap).wait()
        for block in range(0, 128, 32):
            rows = slice(block, block + 32)
            f0, f4, r1, i1, r2, i2, r3, i3 = hue_fourier([raw[tap, k, rows, :].astype(F32) for k in range(8)])
            parts = [f0 * 0.0625, f4 * 0.0625] + [part * 0.125 for part in (r1, i1, r2, i2, r3, i3)]
            for number, part in enumerate(parts):
                ahead[tap, number, rows, :] = part.astype(BF16)
        for number in (0, 1):
            back[tap, number] = ahead[tap, number].T
        for f in (1, 2, 3):
            back[tap, 3 * f - 1] = ahead[tap, 2 * f].T
            im = ahead[tap, 2 * f + 1].T
            back[tap, 3 * f] = -im
            back[tap, 3 * f + 1] = im
        store(tap).start()
        return 0

    lax.fori_loop(0, 9, work, 0)
    for tap in range(9):
        store(tap).wait()


def tap_mask(dy, dx):
    lane = iota((1, 128), 1)
    x, y = lane % 8 + dx, (lane // 8) % 8 + dy
    return (x >= 0) & (x < 8) & (y >= 0) & (y < 8)


def shifted(value, by):
    return value if by % 128 == 0 else pltpu.roll(value, (-by) % 128, 1)


def main_kernel(
    class_rows, got_ref, ahead_ref, forward_ref, backward_ref, fields_ref, class_ref, mean_ref, back_hbm,
    margin_ref, grad_ref,
    turned_ref, minus_ref, key_ref, att_ref, turn_ref, pg_ref, place_ref, slot_ref,
    lift_ref, slope_ref, act_first, act_ref, act_back, mix_ref, mix_next, mix_back, back_ref, sum_ref, count_ref, pool_ref, back_sem,
):
    total, table = got_ref.shape[0] * ROWS, got_ref.shape[0] * 8
    back_copy = pltpu.make_async_copy(back_hbm, turned_ref, back_sem)
    back_copy.start()
    got = got_ref[...].reshape(total, 128)
    picker = (iota((8, 128), 1) == INFO + iota((8, 128), 0)).astype(BF16)
    slot_rows = got_ref[:, 0:16].astype(F32)[:, 0:8].reshape(table, 128).astype(BF16)
    facts = dot(picker, slot_rows, NT)
    spot = iota((1, table), 1)
    is_slot = spot % 2 == 1
    me = facts[6:7]
    live = is_slot & (facts[2:3] > 0.5)
    mine = live & (facts[0:1] == me)
    here = live & ((spot // 8).astype(F32) == me)
    marks = jnp.concatenate([mine.astype(F32), here.astype(F32), jnp.zeros((6, table), F32)], axis=0)
    before = (iota((128, 128), 0) < iota((128, 128), 1)).astype(BF16)
    carry, ranks = jnp.zeros((8, 1), F32), []
    for block in range(table // 128):
        part = marks[:, block * 128 : block * 128 + 128]
        ranks.append(dot(part.astype(BF16), before, NN) + carry)
        carry = carry + jnp.sum(part, axis=1, keepdims=True)
    ranks = jnp.concatenate(ranks, axis=1)
    owned, slots = carry[0:1], carry[1:2]
    key_mine = jnp.where(mine, ranks[0:1], -1.0)
    key_here = jnp.where(here, ranks[1:2] + owned, -1.0)
    key_ref[...] = jnp.concatenate([key_mine, key_here, jnp.full((6, table), -1.0, F32)], axis=0)
    owned_count = jnp.sum(owned).astype(jnp.int32)
    pairs = (owned_count + 1) // 2
    all_pairs = (owned_count + jnp.sum(slots).astype(jnp.int32) + 1) // 2

    for tap in range(9):
        for f in (1, 2, 3):
            minus_ref[tap, f - 1] = -ahead_ref[tap, 2 * f + 1]
    sum_ref[...] = jnp.zeros_like(sum_ref)
    count_ref[...] = jnp.zeros_like(count_ref)
    for ref in (act_first, act_ref, act_back):
        ref[:, 0:16, :] = jnp.zeros((3, 16, 1024), BF16)
        ref[:, 144:160, :] = jnp.zeros((3, 16, 1024), BF16)

    def gather(first_pair):
        height = GROUP * 4
        lane = iota((height, 128), 1)
        odd = iota((height, 128), 0) % 8 >= 4
        colour = iota((height, 128), 0) % 4
        item = (2 * first_pair + 2 * (iota((height, 1), 0) // 8) + (iota((height, 1), 0) % 8) // 4).astype(F32)
        keys = key_ref[...]
        earlier = pltpu.roll(keys, table - 1, 1)
        second = ((keys[0:1] == item) | (keys[1:2] == item)).astype(BF16)
        first = ((earlier[0:1] == item) | (earlier[1:2] == item)).astype(BF16)
        rows2 = dot(second, slot_rows, NN)
        rows1 = dot(first, slot_rows, NN)
        owner, step, label, slot, half = [rows2[:, INFO + i : INFO + i + 1] for i in (0, 1, 3, 4, 5)]
        owns = item < owned
        source = jnp.where(owns, float(total) + step, owner * float(ROWS) + step + 8.0)
        again = jnp.where(owns, source + 12.0, -1.0)
        number = iota((1, total + 128), 1).astype(F32)
        picks = ((number == source) | (number == again)).astype(BF16)
        angle = dot(picks[:, 0:total], got, NN) + dot(picks[:, total:], fields_ref[...], NN)
        angle = jnp.where((half > 0.5) == odd, angle, pltpu.roll(angle, PIX, 1))
        turned1, turned2 = pltpu.roll(rows1, PIX, 1), pltpu.roll(rows2, PIX, 1)
        red = jnp.where(odd, turned1, rows1)
        green = jnp.where(odd, rows1, turned1)
        blue = jnp.where(odd, turned2, rows2)
        own = jnp.where(colour == 0, red, jnp.where(colour == 1, green, blue))
        cross = SKEW * jnp.where(colour == 0, blue - green, jnp.where(colour == 1, red - blue, green - red))
        grey = (red + green + blue) * (1.0 / 3.0)
        sin, cos = sin_cos(angle, angle * angle)
        valid = (colour < 3) & ((lane >= PIX) == odd)
        shade = own - grey
        attacked = jnp.where(valid, grey + cos * shade + sin * cross, 0.0).reshape(GROUP // 2, 8, 128)
        turning = jnp.where(valid, cos * cross - sin * shade, 0.0).reshape(GROUP // 2, 8, 128)
        labels = iota((1, 128), 1).astype(F32)
        classes = float(class_rows)
        named = (labels == label) | (labels == label + classes) | (labels == label + 2.0 * classes)
        gain = PIX * (mean_ref[...] - dot(named.astype(BF16), class_ref[...], NN))
        place = jnp.where(owns, 2.0 * step + half, -1.0)
        spots = pl.ds(first_pair, GROUP // 2)
        att_ref[spots] = attacked + pltpu.roll(attacked, 4, 1)
        turn_ref[spots] = turning + pltpu.roll(turning, 4, 1)
        pg_ref[spots] = gain.reshape(GROUP // 2, 8, 128)
        place_ref[spots] = jnp.broadcast_to(place, (height, 128)).reshape(GROUP // 2, 8, 128)
        slot = jnp.where((item >= owned) & (item < owned + slots), slot, -1.0)
        slot_ref[spots] = jnp.broadcast_to(slot, (height, 128)).reshape(GROUP // 2, 8, 128)

    inner_less = jnp.where(iota((16, 128), 0) % 8 == 0, 0.0, 1.0).astype(BF16)
    inner_more = jnp.where(iota((16, 128), 0) % 8 == 7, 0.0, 1.0).astype(BF16)

    def put(act, y, number, value):
        turns = value.reshape(2, 8, 128)
        less = pltpu.roll(turns, 1, 1).reshape(16, 128).astype(BF16) * inner_less
        more = pltpu.roll(turns, 7, 1).reshape(16, 128).astype(BF16) * inner_more
        for which, part in enumerate((less, value.astype(BF16), more)):
            act[which, 16 * y + 16 : 16 * y + 32, 128 * number : 128 * number + 128] = part

    identity = (iota((128, 128), 0) == iota((128, 128), 1)).astype(BF16)

    def lift(pair, act, slope):
        def start():
            value = att_ref[pair]
            upper = value.astype(BF16).astype(F32)
            value = jnp.where(iota((8, 128), 0) < 4, upper, value - upper)
            taps = [
                jnp.where(tap_mask(tap // 3 - 1, tap % 3 - 1), shifted(value, 8 * (tap // 3 - 1) + tap % 3 - 1), 0.0)
                for tap in range(9)
            ]
            patches = jnp.concatenate(taps + taps, axis=0).astype(BF16)
            turned = dot(identity, patches, NT).astype(BF16)
            lift_ref[...] = dot(turned, forward_ref[...], NN).reshape(2, 8, 8, 384)

        def line(y):
            lifted = lift_ref[:, y].reshape(16, 384)
            g, p, q = lifted[:, 0:128], lifted[:, 128:256], lifted[:, 256:384]
            minus, plus = (p - q) * HALF, (p + q) * HALF
            hues = [g + p, g + minus, g - q, g - plus, g - p, g - minus, g + q, g + plus]
            activated = []
            for k, h in enumerate(hues):
                t = jnp.tanh(h)
                one = 1.0 + t
                value = h * one
                slope_ref[slope, 16 * y : 16 * y + 16, 128 * k : 128 * k + 128] = one + value * (1.0 - t)
                activated.append(value)
            for number, part in enumerate(hue_fourier(activated)):
                put(act, y, number, part)

        return [start] + [functools.partial(line, y) for y in range(8)]

    def convolve(act, out, forward, thirds=False):
        def moved(tap, columns):
            dy, dx = (tap // 3, tap % 3) if forward else (2 - tap // 3, 2 - tap % 3)
            return act[dx, 16 * dy : 16 * dy + 128, columns]

        weights = ahead_ref if forward else turned_ref

        sums = {}

        def part(f, taps):
            columns = slice(256 * f, 256 * f + 256)
            right = []
            for tap in taps:
                if f == 0:
                    zero = jnp.zeros((128, 128), BF16)
                    square = ((weights[tap, 0], zero), (zero, weights[tap, 1]))
                elif forward:
                    re, im, minus = weights[tap, 2 * f], weights[tap, 2 * f + 1], minus_ref[tap, f - 1]
                    square = ((re, minus), (im, re))
                else:
                    re, minus, im = [weights[tap, 3 * f - 1 + i] for i in range(3)]
                    square = ((re, im), (minus, re))
                right += [jnp.concatenate(pieces, axis=1) for pieces in square]
            left = jnp.concatenate([moved(tap, columns) for tap in taps], axis=1)
            result = dot(left, jnp.concatenate(right, axis=0), NN)
            sums[f] = sums[f] + result if f in sums else result
            if taps[-1] == 8:
                out[:, columns] = sums[f]

        if thirds:
            return [
                functools.partial(part, f, range(3 * third, 3 * third + 3))
                for both in ((0, 1), (2, 3)) for third in range(3) for f in both
            ]
        return [functools.partial(part, f, range(9)) for f in range(4)]

    def gains(pair):
        return [pg_ref[pair][4 * t : 4 * t + 1] for t in range(2)]

    def add_up(pair, y, values):
        while len(values) > 1:
            values = [a + b for a, b in zip(values[::2], values[1::2])]
        pool_ref[pair] = values[0] if y == 0 else pool_ref[pair] + values[0]

    def slopes(pair, mix, before=None):
        spread = jnp.concatenate([jnp.broadcast_to(g, (8, 128)) for g in gains(pair)], axis=0) * (0.5 / 512.0)

        def line(y):
            parts = [mix[16 * y : 16 * y + 16, 128 * k : 128 * k + 128] for k in range(8)]
            slope, values = [], []
            for h in hue_inverse(parts):
                t = jnp.tanh(h)
                one = 1.0 + t
                value = h * one
                values.append(value)
                slope.append((one + value * (1.0 - t)) * spread)
            add_up(pair, y, values)
            for number, part in enumerate(hue_fourier(slope)):
                put(act_back, y, number, part)
            for row, f in (before or {}).get(y, ()):
                columns = slice(256 * f, 256 * f + 128)
                act_ref[1, row : row + 16, columns] = jnp.minimum(jnp.maximum(part, 0.0), 0.0).astype(BF16)

        return [functools.partial(line, y) for y in range(8)]

    def pool(pair, mix):
        def line(y):
            parts = [mix[16 * y : 16 * y + 16, 128 * k : 128 * k + 128] for k in range(8)]
            add_up(pair, y, [h * (1.0 + jnp.tanh(h)) for h in hue_inverse(parts)])

        return [functools.partial(line, y) for y in range(8)]

    def margins(pair, wanted):
        pooled = jnp.sum(pool_ref[pair].reshape(2, 8, 128), axis=1)
        gain = jnp.concatenate(gains(pair), axis=0)
        margin = jnp.sum(pooled * gain, axis=1, keepdims=True) * (-1.0 / (PIX * 512.0))
        at = jnp.where(wanted, slot_ref[pair], -1.0)
        lanes = iota((1, 128), 1).astype(F32)
        return sum(jnp.where(lanes == at[4 * t : 4 * t + 1], margin[t : t + 1], 0.0) for t in range(2))

    def back(pair, slope, wanted):
        def line(y):
            parts = [mix_back[16 * y : 16 * y + 16, 128 * k : 128 * k + 128] for k in range(8)]
            grads = [
                part * slope_ref[slope, 16 * y : 16 * y + 16, 128 * k : 128 * k + 128]
                for k, part in enumerate(hue_inverse(parts))
            ]
            s = [grads[i] + grads[i + 4] for i in range(4)]
            d = [grads[i] - grads[i + 4] for i in range(4)]
            minus, plus = (d[1] - d[3]) * HALF, (d[1] + d[3]) * HALF
            for i, value in enumerate(((s[0] + s[2]) + (s[1] + s[3]), d[0] + minus, -d[2] - plus)):
                upper = value.astype(BF16).astype(F32)
                for place, part in ((i, upper), (i + 3, value - upper), (i + 6, upper)):
                    back_ref[:, y, :, 128 * place : 128 * place + 128] = part.reshape(2, 8, 128)

        def finish():
            gradient = dot(backward_ref[...], back_ref[...].reshape(128, 1152).astype(BF16), NT)
            number_of = (2 * iota((16, 128), 0) + iota((16, 128), 1) // PIX).astype(F32)
            colour_grad = jnp.zeros((8, 128), F32)
            for tap in range(9):
                dy, dx = tap // 3 - 1, tap % 3 - 1
                part = gradient[8 * tap : 8 * tap + 8]
                colour_grad += jnp.where(tap_mask(-dy, -dx), shifted(part, -8 * dy - dx), 0.0)
            angle_grad = jnp.sum(colour_grad * turn_ref[pair], axis=0, keepdims=True)
            turned = pltpu.roll(jnp.broadcast_to(angle_grad, (8, 128)), PIX, 1)[0:1]
            places = jnp.where(wanted, place_ref[pair], -1.0)
            for t in range(2):
                chosen = jnp.where((iota((1, 128), 1) >= PIX) == (t == 1), angle_grad, turned)
                same = number_of == places[4 * t : 4 * t + 1]
                sum_ref[...] += jnp.where(same, chosen, 0.0)
                count_ref[...] += same.astype(F32)

        return [functools.partial(line, y) for y in range(8)] + [finish]

    def together(*lists):
        longest = max(len(steps) for steps in lists)
        for place in range(longest):
            for steps in lists:
                for number in range(len(steps) * place // longest, len(steps) * (place + 1) // longest):
                    steps[number]()

    gather(0)
    together(lift(0, act_first, 0))
    together(convolve(act_first, mix_ref, True), lift(1, act_ref, 1))
    back_copy.wait()

    def copy_mix(y):
        mix_ref[16 * y : 16 * y + 16] = mix_next[16 * y : 16 * y + 16]

    def step(pair, _):
        after = pair + 2

        @pl.when((after % (GROUP // 2) == 0) & (after < pairs + 2))
        def _():
            gather(after)

        earlier = jnp.maximum(pair - 1, 0)
        parts = convolve(act_ref, mix_next, True, True)
        lines = slopes(pair, mix_ref, {1: [(144, 0), (144, 1)], 3: [(0, 2), (0, 3)], 5: [(144, 2)], 7: [(144, 3)]})
        ends = back(earlier, earlier % 4, pair > 0)
        for kind, number in [(0, 0), (0, 1), (0, 2), (0, 3), (1, 0), (1, 1), (0, 4), (0, 5), (1, 2), (1, 3), (0, 6), (0, 7), (0, 8), (0, 9), (1, 4), (1, 5), (0, 10), (1, 6), (1, 7), (0, 11), *((2, i) for i in range(9))]:
            (parts, lines, ends)[kind][number]()
        together(
            convolve(act_back, mix_back, False),
            lift(after, act_ref, after % 4),
            [functools.partial(copy_mix, y) for y in range(8)],
        )
        return 0

    lax.fori_loop(0, pairs, step, 0)
    last = jnp.maximum(pairs - 1, 0)

    @pl.when(all_pairs - pairs > 1)
    def _():
        together(
            convolve(act_ref, mix_next, True), back(last, last % 4, pairs > 0), pool(pairs, mix_ref)
        )
        together(pool(pairs + 1, mix_next))

    @pl.when(all_pairs - pairs <= 1)
    def _():
        together(back(last, last % 4, pairs > 0), pool(pairs, mix_ref))

    result = margins(last, pairs > 0) + margins(pairs, all_pairs > pairs) + margins(pairs + 1, all_pairs > pairs + 1)
    margin_ref[...] = result[0, 0 : margin_ref.shape[0]]
    grad_ref[...] = (sum_ref[...] / jnp.maximum(count_ref[...], 1.0))[0 : grad_ref.shape[0]]


def sin_cos(angle, square):
    sin = -1.0 / 39916800.0
    for coefficient in (1.0 / 362880.0, -1.0 / 5040.0, 1.0 / 120.0, -1.0 / 6.0, 1.0):
        sin = sin * square + coefficient
    cos = 1.0 / 479001600.0
    for coefficient in (-1.0 / 3628800.0, 1.0 / 40320.0, -1.0 / 720.0, 1.0 / 24.0, -0.5, 1.0):
        cos = cos * square + coefficient
    return sin * angle, cos


def vmem(count):
    return [pl.BlockSpec(memory_space=pltpu.VMEM) for _ in range(count)]


def in_hbm(array):
    return pltpu.with_memory_space_constraint(array, pltpu.HBM)


def shards(
    tiles, tile_slide, tile_mask, tile_label, attack_field, lift_weight, group_weight, class_weight
):
    devices = lax.axis_size("tiles")
    field = attack_field.reshape(-1, 128)
    slides = attack_field.shape[0] // PIX
    message = pl.pallas_call(
        functools.partial(pack_kernel, slides),
        out_shape=jax.ShapeDtypeStruct((devices, ROWS, 128), BF16),
        in_specs=[pl.BlockSpec(memory_space=pltpu.SMEM)] * 3 + vmem(2),
        out_specs=pl.BlockSpec(memory_space=pltpu.VMEM),
        name="pack",
    )(tile_slide, tile_mask, tile_label, tiles, field)
    got = lax.all_to_all(message, "tiles", split_axis=0, concat_axis=0, tiled=True)
    hbm = pl.BlockSpec(memory_space=pltpu.HBM)
    ahead, turned, forward, backward, fields, classes, mean = pl.pallas_call(
        weight_kernel,
        out_shape=(
            jax.ShapeDtypeStruct((9, 8, 128, 128), BF16),
            pltpu.HBM((9, 11, 128, 128), BF16),
            jax.ShapeDtypeStruct((144, 384), BF16),
            jax.ShapeDtypeStruct((80, 1152), BF16),
            jax.ShapeDtypeStruct((128, 128), BF16),
            jax.ShapeDtypeStruct((128, 128), BF16),
            jax.ShapeDtypeStruct((1, 128), F32),
        ),
        in_specs=[hbm] * 4,
        out_specs=(*vmem(1), hbm, *vmem(5)),
        scratch_shapes=[
            pltpu.VMEM((9, 8, 128, 128), BF16),
            pltpu.VMEM((9, 3, 128), F32),
            pltpu.VMEM(field.shape, F32),
            pltpu.VMEM(class_weight.shape[::-1], F32),
            pltpu.VMEM((9, 11, 128, 128), BF16),
            pltpu.SemaphoreType.DMA((9,)),
            pltpu.SemaphoreType.DMA((3,)),
            pltpu.SemaphoreType.DMA((9,)),
        ],
        compiler_params=pltpu.CompilerParams(vmem_limit_bytes=16 * 2**20),
        cost_estimate=pl.CostEstimate(flops=10_000_000, bytes_accessed=9_000_000, transcendentals=0),
        name="weights",
    )(in_hbm(group_weight), in_hbm(lift_weight), in_hbm(field), in_hbm(class_weight.T))
    spots = devices + SLOTS // 2 + GROUP // 2
    margins, attack_grad = pl.pallas_call(
        functools.partial(main_kernel, class_weight.shape[1]),
        out_shape=(jax.ShapeDtypeStruct(tile_slide.shape, F32), jax.ShapeDtypeStruct(field.shape, F32)),
        in_specs=vmem(7) + [hbm],
        out_specs=tuple(vmem(2)),
        scratch_shapes=[
            pltpu.VMEM((9, 11, 128, 128), BF16),
            pltpu.VMEM((9, 3, 128, 128), BF16),
            pltpu.VMEM((8, devices * 8), F32),
            *[pltpu.VMEM((spots, 8, 128), F32) for _ in range(5)],
            pltpu.VMEM((2, 8, 8, 384), F32),
            pltpu.VMEM((4, 128, 1024), F32),
            *[pltpu.VMEM((3, 160, 1024), BF16) for _ in range(3)],
            *[pltpu.VMEM((128, 1024), F32) for _ in range(3)],
            pltpu.VMEM((2, 8, 8, 1152), F32),
            pltpu.VMEM((16, 128), F32),
            pltpu.VMEM((16, 128), F32),
            pltpu.VMEM((spots, 16, 128), F32),
            pltpu.SemaphoreType.DMA,
        ],
        compiler_params=pltpu.CompilerParams(vmem_limit_bytes=32 * 2**20),
        cost_estimate=pl.CostEstimate(flops=4_000_000_000, bytes_accessed=9_000_000, transcendentals=2_000_000),
        name="attack",
    )(got, ahead, forward, backward, fields, classes, mean, in_hbm(turned))
    return (margins, attack_grad.reshape(-1))


def solution(mesh):
    return jax.shard_map(
        shards,
        mesh=mesh,
        in_specs=(
            P(None, ("groups", "tiles")),
            P(("groups", "tiles")),
            P(("groups", "tiles")),
            P(("groups", "tiles")),
            P(("groups", "tiles")),
            P(),
            P(),
            P(),
        ),
        out_specs=(P(("groups", "tiles")), P(("groups", "tiles"))),
        check_vma=False,
    )
```

```python
import functools
import math

import jax
import jax.numpy as jnp
from jax import lax
from jax.experimental import pallas as pl
from jax.experimental.pallas import tpu as pltpu
from jax.sharding import PartitionSpec as P

F32 = jnp.float32
BF16 = jnp.bfloat16
PIX = 64
ROWS = 24
INFO = 64
SLOTS = 4
GROUP = 12
SKEW = 1.0 / math.sqrt(3.0)
HALF = math.sqrt(0.5)


def iota(shape, axis):
    return lax.broadcasted_iota(jnp.int32, shape, axis)


def dot(a, b, dims, precision=None):
    return lax.dot_general(a, b, (dims, ((), ())), precision=precision, preferred_element_type=F32)


NN = ((1,), (0,))
NT = ((1,), (1,))
TN = ((0,), (0,))


def hue_fourier(x):
    s = [x[i] + x[i + 4] for i in range(4)]
    d = [x[i] - x[i + 4] for i in range(4)]
    e, o = s[0] + s[2], s[1] + s[3]
    dm, dp = (d[1] - d[3]) * HALF, (d[1] + d[3]) * HALF
    return [e + o, e - o, d[0] + dm, -d[2] - dp, s[0] - s[2], s[3] - s[1], d[0] - dm, d[2] - dp]


def hue_inverse(c):
    f0, f4, r1, i1, r2, i2, r3, i3 = c
    a, b = f0 + f4, f0 - f4
    s0, s2, s1, s3 = a + r2, a - r2, b - i2, b + i2
    d0, d2 = r1 + r3, i3 - i1
    p, q = (r1 - r3) * HALF, (i1 + i3) * HALF
    d1, d3 = p - q, -p - q
    s, d = (s0, s1, s2, s3), (d0, d1, d2, d3)
    return [s[k] + d[k] for k in range(4)] + [s[k] - d[k] for k in range(4)]


def pack_kernel(slides, slide_ref, mask_ref, label_ref, tiles_ref, field_ref, out_ref):
    lane = iota((1, 128), 1)
    left = lane < PIX
    tiles = tiles_ref[...].astype(F32)
    rows, parts = [], []
    for slot in range(4):
        part = tiles[:, 128 * (slot // 2) : 128 * (slot // 2) + 128]
        turned = pltpu.roll(part, PIX, 1)
        low, high = (part, turned) if slot % 2 == 0 else (turned, part)
        slide = slide_ref[slot]
        owner = slide // slides
        place = slide - owner * slides
        facts = [owner, place // 2, mask_ref[slot], label_ref[slot], slot, place % 2]
        info = jnp.zeros((1, 128), jnp.int32)
        for number, fact in enumerate(facts):
            info = jnp.where(lane == INFO + number, fact, info)
        rows.append(jnp.where(left, low[0:1], high[1:2]))
        rows.append(jnp.where(left, low[2:3], info.astype(F32)))
    rows = jnp.concatenate(rows, axis=0)
    rest = jnp.concatenate([field_ref[...], jnp.zeros((4, 128), F32)], axis=0)
    at = (iota((8, 128), 1) == INFO + 6) & (iota((8, 128), 0) % 2 == 1)
    for target in range(out_ref.shape[0]):
        slot_rows = jnp.where(at, float(target), rows)
        out_ref[target] = jnp.concatenate([slot_rows, rest], axis=0).astype(BF16)


def weight_kernel(
    weight_hbm, lift_hbm, field_hbm, class_hbm,
    ahead, back_hbm, forward_ref, backward_ref, fields_ref, parts_ref, mean_ref,
    raw, lift_ref, field_ref, class_ref, back, in_sem, small_sem, out_sem,
):
    def fetch(tap):
        return pltpu.make_async_copy(weight_hbm.at[:, tap], raw.at[tap], in_sem.at[tap])

    def store(tap):
        return pltpu.make_async_copy(back.at[tap], back_hbm.at[tap], out_sem.at[tap])

    small = [
        pltpu.make_async_copy(source, target, small_sem.at[number])
        for number, (source, target) in enumerate(
            ((lift_hbm, lift_ref), (field_hbm, field_ref), (class_hbm, class_ref))
        )
    ]
    for copy in small:
        copy.start()
    for tap in range(9):
        fetch(tap).start()
    for copy in small:
        copy.wait()
    field = field_ref[...]
    upper = field.astype(BF16).astype(F32)
    fields_ref[...] = jnp.concatenate([upper, field - upper, jnp.zeros((104, 128), F32)], axis=0).astype(BF16)
    weight = class_ref[...]
    upper = weight.astype(BF16).astype(F32)
    middle = (weight - upper).astype(BF16).astype(F32)
    empty = jnp.zeros((128 - 3 * weight.shape[0], 128), F32)
    parts_ref[...] = jnp.concatenate([upper, middle, weight - upper - middle, empty], axis=0).astype(BF16)
    mean_ref[...] = jnp.mean(weight, axis=0, keepdims=True)

    both, single = [], []
    for tap in range(9):
        lift = lift_ref[tap]
        l0, l1, l2 = lift[0:1], lift[1:2], lift[2:3]
        grey = (l0 + l1 + l2) * (1.0 / 3.0)
        zero = jnp.zeros((1, 128), F32)
        columns = (
            [grey] * 3,
            [l0 - grey, l1 - grey, l2 - grey],
            [(l1 - l2) * SKEW, (l2 - l0) * SKEW, (l0 - l1) * SKEW],
        )
        both.append(jnp.concatenate([jnp.concatenate([*c, zero, *c, zero], axis=0) for c in columns], axis=1))
        single.append(jnp.concatenate([jnp.concatenate([*c, *[zero] * 5], axis=0) for c in columns], axis=1))
    both = jnp.concatenate(both, axis=0) * 0.5
    upper = both.astype(BF16).astype(F32)
    forward_ref[...] = jnp.concatenate([upper, both - upper], axis=0).astype(BF16)
    single = jnp.concatenate(single + [jnp.zeros((8, 384), F32)], axis=0)
    upper = single.astype(BF16).astype(F32)
    backward_ref[...] = jnp.concatenate([upper, upper, single - upper], axis=1).astype(BF16)

    def work(tap, _):
        fetch(tap).wait()
        for block in range(0, 128, 32):
            rows = slice(block, block + 32)
            f0, f4, r1, i1, r2, i2, r3, i3 = hue_fourier([raw[tap, k, rows, :].astype(F32) for k in range(8)])
            parts = [f0 * 0.0625, f4 * 0.0625] + [part * 0.125 for part in (r1, i1, r2, i2, r3, i3)]
            for number, part in enumerate(parts):
                ahead[tap, number, rows, :] = part.astype(BF16)
        for number in (0, 1):
            back[tap, number] = ahead[tap, number].T
        for f in (1, 2, 3):
            back[tap, 3 * f - 1] = ahead[tap, 2 * f].T
            im = ahead[tap, 2 * f + 1].T
            back[tap, 3 * f] = -im
            back[tap, 3 * f + 1] = im
        store(tap).start()
        return 0

    lax.fori_loop(0, 9, work, 0)
    for tap in range(9):
        store(tap).wait()


def tap_mask(dy, dx):
    lane = iota((1, 128), 1)
    x, y = lane % 8 + dx, (lane // 8) % 8 + dy
    return (x >= 0) & (x < 8) & (y >= 0) & (y < 8)


def shifted(value, by):
    return value if by % 128 == 0 else pltpu.roll(value, (-by) % 128, 1)


def main_kernel(
    class_rows, got_ref, ahead_ref, forward_ref, backward_ref, fields_ref, class_ref, mean_ref, back_hbm,
    margin_ref, grad_ref,
    turned_ref, minus_ref, key_ref, att_ref, turn_ref, pg_ref, place_ref, slot_ref,
    lift_ref, slope_ref, act_first, act_ref, act_back, mix_ref, mix_next, mix_back, back_ref, sum_ref, count_ref, pool_ref, back_sem,
):
    total, table = got_ref.shape[0] * ROWS, got_ref.shape[0] * 8
    back_copy = pltpu.make_async_copy(back_hbm, turned_ref, back_sem)
    back_copy.start()
    got = got_ref[...].reshape(total, 128)
    picker = (iota((8, 128), 1) == INFO + iota((8, 128), 0)).astype(BF16)
    slot_rows = got_ref[:, 0:16].astype(F32)[:, 0:8].reshape(table, 128).astype(BF16)
    facts = dot(picker, slot_rows, NT)
    spot = iota((1, table), 1)
    is_slot = spot % 2 == 1
    me = facts[6:7]
    live = is_slot & (facts[2:3] > 0.5)
    mine = live & (facts[0:1] == me)
    here = live & ((spot // 8).astype(F32) == me)
    marks = jnp.concatenate([mine.astype(F32), here.astype(F32), jnp.zeros((6, table), F32)], axis=0)
    before = (iota((128, 128), 0) < iota((128, 128), 1)).astype(BF16)
    carry, ranks = jnp.zeros((8, 1), F32), []
    for block in range(table // 128):
        part = marks[:, block * 128 : block * 128 + 128]
        ranks.append(dot(part.astype(BF16), before, NN) + carry)
        carry = carry + jnp.sum(part, axis=1, keepdims=True)
    ranks = jnp.concatenate(ranks, axis=1)
    owned, slots = carry[0:1], carry[1:2]
    key_mine = jnp.where(mine, ranks[0:1], -1.0)
    key_here = jnp.where(here, ranks[1:2] + owned, -1.0)
    key_ref[...] = jnp.concatenate([key_mine, key_here, jnp.full((6, table), -1.0, F32)], axis=0)
    owned_count = jnp.sum(owned).astype(jnp.int32)
    pairs = (owned_count + 1) // 2
    all_pairs = (owned_count + jnp.sum(slots).astype(jnp.int32) + 1) // 2

    for tap in range(9):
        for f in (1, 2, 3):
            minus_ref[tap, f - 1] = -ahead_ref[tap, 2 * f + 1]
    sum_ref[...] = jnp.zeros_like(sum_ref)
    count_ref[...] = jnp.zeros_like(count_ref)
    for ref in (act_first, act_ref, act_back):
        ref[:, 0:16, :] = jnp.zeros((3, 16, 1024), BF16)
        ref[:, 144:160, :] = jnp.zeros((3, 16, 1024), BF16)

    def gather(first_pair):
        height = GROUP * 4
        lane = iota((height, 128), 1)
        odd = iota((height, 128), 0) % 8 >= 4
        colour = iota((height, 128), 0) % 4
        item = (2 * first_pair + 2 * (iota((height, 1), 0) // 8) + (iota((height, 1), 0) % 8) // 4).astype(F32)
        keys = key_ref[...]
        earlier = pltpu.roll(keys, table - 1, 1)
        second = ((keys[0:1] == item) | (keys[1:2] == item)).astype(BF16)
        first = ((earlier[0:1] == item) | (earlier[1:2] == item)).astype(BF16)
        rows2 = dot(second, slot_rows, NN)
        rows1 = dot(first, slot_rows, NN)
        owner, step, label, slot, half = [rows2[:, INFO + i : INFO + i + 1] for i in (0, 1, 3, 4, 5)]
        owns = item < owned
        source = jnp.where(owns, float(total) + step, owner * float(ROWS) + step + 8.0)
        again = jnp.where(owns, source + 12.0, -1.0)
        number = iota((1, total + 128), 1).astype(F32)
        picks = ((number == source) | (number == again)).astype(BF16)
        angle = dot(picks[:, 0:total], got, NN) + dot(picks[:, total:], fields_ref[...], NN)
        angle = jnp.where((half > 0.5) == odd, angle, pltpu.roll(angle, PIX, 1))
        turned1, turned2 = pltpu.roll(rows1, PIX, 1), pltpu.roll(rows2, PIX, 1)
        red = jnp.where(odd, turned1, rows1)
        green = jnp.where(odd, rows1, turned1)
        blue = jnp.where(odd, turned2, rows2)
        own = jnp.where(colour == 0, red, jnp.where(colour == 1, green, blue))
        cross = SKEW * jnp.where(colour == 0, blue - green, jnp.where(colour == 1, red - blue, green - red))
        grey = (red + green + blue) * (1.0 / 3.0)
        sin, cos = sin_cos(angle, angle * angle)
        valid = (colour < 3) & ((lane >= PIX) == odd)
        shade = own - grey
        attacked = jnp.where(valid, grey + cos * shade + sin * cross, 0.0).reshape(GROUP // 2, 8, 128)
        turning = jnp.where(valid, cos * cross - sin * shade, 0.0).reshape(GROUP // 2, 8, 128)
        labels = iota((1, 128), 1).astype(F32)
        classes = float(class_rows)
        named = (labels == label) | (labels == label + classes) | (labels == label + 2.0 * classes)
        gain = PIX * (mean_ref[...] - dot(named.astype(BF16), class_ref[...], NN))
        place = jnp.where(owns, 2.0 * step + half, -1.0)
        spots = pl.ds(first_pair, GROUP // 2)
        att_ref[spots] = attacked + pltpu.roll(attacked, 4, 1)
        turn_ref[spots] = turning + pltpu.roll(turning, 4, 1)
        pg_ref[spots] = gain.reshape(GROUP // 2, 8, 128)
        place_ref[spots] = jnp.broadcast_to(place, (height, 128)).reshape(GROUP // 2, 8, 128)
        slot = jnp.where((item >= owned) & (item < owned + slots), slot, -1.0)
        slot_ref[spots] = jnp.broadcast_to(slot, (height, 128)).reshape(GROUP // 2, 8, 128)

    inner_less = jnp.where(iota((16, 128), 0) % 8 == 0, 0.0, 1.0).astype(BF16)
    inner_more = jnp.where(iota((16, 128), 0) % 8 == 7, 0.0, 1.0).astype(BF16)

    def put(act, y, number, value):
        turns = value.reshape(2, 8, 128)
        less = pltpu.roll(turns, 1, 1).reshape(16, 128).astype(BF16) * inner_less
        more = pltpu.roll(turns, 7, 1).reshape(16, 128).astype(BF16) * inner_more
        for which, part in enumerate((less, value.astype(BF16), more)):
            act[which, 16 * y + 16 : 16 * y + 32, 128 * number : 128 * number + 128] = part

    identity = (iota((128, 128), 0) == iota((128, 128), 1)).astype(BF16)

    def lift(pair, act, slope):
        def start():
            value = att_ref[pair]
            upper = value.astype(BF16).astype(F32)
            value = jnp.where(iota((8, 128), 0) < 4, upper, value - upper)
            taps = [
                jnp.where(tap_mask(tap // 3 - 1, tap % 3 - 1), shifted(value, 8 * (tap // 3 - 1) + tap % 3 - 1), 0.0)
                for tap in range(9)
            ]
            patches = jnp.concatenate(taps + taps, axis=0).astype(BF16)
            turned = dot(identity, patches, NT).astype(BF16)
            lift_ref[...] = dot(turned, forward_ref[...], NN).reshape(2, 8, 8, 384)

        def line(y):
            lifted = lift_ref[:, y].reshape(16, 384)
            g, p, q = lifted[:, 0:128], lifted[:, 128:256], lifted[:, 256:384]
            minus, plus = (p - q) * HALF, (p + q) * HALF
            hues = [g + p, g + minus, g - q, g - plus, g - p, g - minus, g + q, g + plus]
            activated = []
            for k, h in enumerate(hues):
                t = jnp.tanh(h)
                one = 1.0 + t
                value = h * one
                slope_ref[slope, 16 * y : 16 * y + 16, 128 * k : 128 * k + 128] = one + value * (1.0 - t)
                activated.append(value)
            for number, part in enumerate(hue_fourier(activated)):
                put(act, y, number, part)

        return [start] + [functools.partial(line, y) for y in range(8)]

    def convolve(act, out, forward, thirds=False):
        def moved(tap, columns):
            dy, dx = (tap // 3, tap % 3) if forward else (2 - tap // 3, 2 - tap % 3)
            return act[dx, 16 * dy : 16 * dy + 128, columns]

        weights = ahead_ref if forward else turned_ref

        sums = {}

        def part(f, taps):
            columns = slice(256 * f, 256 * f + 256)
            right = []
            for tap in taps:
                if f == 0:
                    zero = jnp.zeros((128, 128), BF16)
                    square = ((weights[tap, 0], zero), (zero, weights[tap, 1]))
                elif forward:
                    re, im, minus = weights[tap, 2 * f], weights[tap, 2 * f + 1], minus_ref[tap, f - 1]
                    square = ((re, minus), (im, re))
                else:
                    re, minus, im = [weights[tap, 3 * f - 1 + i] for i in range(3)]
                    square = ((re, im), (minus, re))
                right += [jnp.concatenate(pieces, axis=1) for pieces in square]
            left = jnp.concatenate([moved(tap, columns) for tap in taps], axis=1)
            result = dot(left, jnp.concatenate(right, axis=0), NN)
            sums[f] = sums[f] + result if f in sums else result
            if taps[-1] == 8:
                out[:, columns] = sums[f]

        if thirds:
            return [
                functools.partial(part, f, range(3 * third, 3 * third + 3))
                for both in ((0, 1), (2, 3)) for third in range(3) for f in both
            ]
        return [functools.partial(part, f, range(9)) for f in range(4)]

    def gains(pair):
        return [pg_ref[pair][4 * t : 4 * t + 1] for t in range(2)]

    def add_up(pair, y, values):
        while len(values) > 1:
            values = [a + b for a, b in zip(values[::2], values[1::2])]
        pool_ref[pair] = values[0] if y == 0 else pool_ref[pair] + values[0]

    def slopes(pair, mix, before=None):
        spread = jnp.concatenate([jnp.broadcast_to(g, (8, 128)) for g in gains(pair)], axis=0) * (0.5 / 512.0)

        def line(y):
            parts = [mix[16 * y : 16 * y + 16, 128 * k : 128 * k + 128] for k in range(8)]
            slope, values = [], []
            for h in hue_inverse(parts):
                t = jnp.tanh(h)
                one = 1.0 + t
                value = h * one
                values.append(value)
                slope.append((one + value * (1.0 - t)) * spread)
            add_up(pair, y, values)
            for number, part in enumerate(hue_fourier(slope)):
                put(act_back, y, number, part)
            for row, f in (before or {}).get(y, ()):
                columns = slice(256 * f, 256 * f + 128)
                act_ref[1, row : row + 16, columns] = jnp.minimum(jnp.maximum(part, 0.0), 0.0).astype(BF16)

        return [functools.partial(line, y) for y in range(8)]

    def pool(pair, mix):
        def line(y):
            parts = [mix[16 * y : 16 * y + 16, 128 * k : 128 * k + 128] for k in range(8)]
            add_up(pair, y, [h * (1.0 + jnp.tanh(h)) for h in hue_inverse(parts)])

        return [functools.partial(line, y) for y in range(8)]

    def margins(pair, wanted):
        pooled = jnp.sum(pool_ref[pair].reshape(2, 8, 128), axis=1)
        gain = jnp.concatenate(gains(pair), axis=0)
        margin = jnp.sum(pooled * gain, axis=1, keepdims=True) * (-1.0 / (PIX * 512.0))
        at = jnp.where(wanted, slot_ref[pair], -1.0)
        lanes = iota((1, 128), 1).astype(F32)
        return sum(jnp.where(lanes == at[4 * t : 4 * t + 1], margin[t : t + 1], 0.0) for t in range(2))

    def back(pair, slope, wanted):
        def line(y):
            parts = [mix_back[16 * y : 16 * y + 16, 128 * k : 128 * k + 128] for k in range(8)]
            grads = [
                part * slope_ref[slope, 16 * y : 16 * y + 16, 128 * k : 128 * k + 128]
                for k, part in enumerate(hue_inverse(parts))
            ]
            s = [grads[i] + grads[i + 4] for i in range(4)]
            d = [grads[i] - grads[i + 4] for i in range(4)]
            minus, plus = (d[1] - d[3]) * HALF, (d[1] + d[3]) * HALF
            for i, value in enumerate(((s[0] + s[2]) + (s[1] + s[3]), d[0] + minus, -d[2] - plus)):
                upper = value.astype(BF16).astype(F32)
                for place, part in ((i, upper), (i + 3, value - upper), (i + 6, upper)):
                    back_ref[:, y, :, 128 * place : 128 * place + 128] = part.reshape(2, 8, 128)

        def finish():
            gradient = dot(backward_ref[...], back_ref[...].reshape(128, 1152).astype(BF16), NT)
            number_of = (2 * iota((16, 128), 0) + iota((16, 128), 1) // PIX).astype(F32)
            colour_grad = jnp.zeros((8, 128), F32)
            for tap in range(9):
                dy, dx = tap // 3 - 1, tap % 3 - 1
                part = gradient[8 * tap : 8 * tap + 8]
                colour_grad += jnp.where(tap_mask(-dy, -dx), shifted(part, -8 * dy - dx), 0.0)
            angle_grad = jnp.sum(colour_grad * turn_ref[pair], axis=0, keepdims=True)
            turned = pltpu.roll(jnp.broadcast_to(angle_grad, (8, 128)), PIX, 1)[0:1]
            places = jnp.where(wanted, place_ref[pair], -1.0)
            for t in range(2):
                chosen = jnp.where((iota((1, 128), 1) >= PIX) == (t == 1), angle_grad, turned)
                same = number_of == places[4 * t : 4 * t + 1]
                sum_ref[...] += jnp.where(same, chosen, 0.0)
                count_ref[...] += same.astype(F32)

        return [functools.partial(line, y) for y in range(8)] + [finish]

    def together(*lists):
        longest = max(len(steps) for steps in lists)
        for place in range(longest):
            for steps in lists:
                for number in range(len(steps) * place // longest, len(steps) * (place + 1) // longest):
                    steps[number]()

    gather(0)
    together(lift(0, act_first, 0))
    together(convolve(act_first, mix_ref, True), lift(1, act_ref, 1))
    back_copy.wait()

    def copy_mix(y):
        mix_ref[16 * y : 16 * y + 16] = mix_next[16 * y : 16 * y + 16]

    def step(pair, _):
        after = pair + 2

        @pl.when((after % (GROUP // 2) == 0) & (after < pairs + 2))
        def _():
            gather(after)

        earlier = jnp.maximum(pair - 1, 0)
        parts = convolve(act_ref, mix_next, True, True)
        lines = slopes(pair, mix_ref, {1: [(144, 0), (144, 1)], 3: [(0, 2), (0, 3)], 5: [(144, 2)], 7: [(144, 3)]})
        ends = back(earlier, earlier % 4, pair > 0)
        for kind, number in [*((2, i) for i in range(9)), (0, 0), (0, 1), (0, 2), (0, 3), (1, 0), (1, 1), (0, 4), (0, 5), (1, 2), (1, 3), (0, 6), (0, 7), (0, 8), (0, 9), (1, 4), (1, 5), (0, 10), (1, 6), (1, 7), (0, 11)]:
            (parts, lines, ends)[kind][number]()
        together(
            convolve(act_back, mix_back, False),
            lift(after, act_ref, after % 4),
            [functools.partial(copy_mix, y) for y in range(8)],
        )
        return 0

    lax.fori_loop(0, pairs, step, 0)
    last = jnp.maximum(pairs - 1, 0)

    @pl.when(all_pairs - pairs > 1)
    def _():
        together(
            convolve(act_ref, mix_next, True), back(last, last % 4, pairs > 0), pool(pairs, mix_ref)
        )
        together(pool(pairs + 1, mix_next))

    @pl.when(all_pairs - pairs <= 1)
    def _():
        together(back(last, last % 4, pairs > 0), pool(pairs, mix_ref))

    result = margins(last, pairs > 0) + margins(pairs, all_pairs > pairs) + margins(pairs + 1, all_pairs > pairs + 1)
    margin_ref[...] = result[0, 0 : margin_ref.shape[0]]
    grad_ref[...] = (sum_ref[...] / jnp.maximum(count_ref[...], 1.0))[0 : grad_ref.shape[0]]


def sin_cos(angle, square):
    sin = -1.0 / 39916800.0
    for coefficient in (1.0 / 362880.0, -1.0 / 5040.0, 1.0 / 120.0, -1.0 / 6.0, 1.0):
        sin = sin * square + coefficient
    cos = 1.0 / 479001600.0
    for coefficient in (-1.0 / 3628800.0, 1.0 / 40320.0, -1.0 / 720.0, 1.0 / 24.0, -0.5, 1.0):
        cos = cos * square + coefficient
    return sin * angle, cos


def vmem(count):
    return [pl.BlockSpec(memory_space=pltpu.VMEM) for _ in range(count)]


def in_hbm(array):
    return pltpu.with_memory_space_constraint(array, pltpu.HBM)


def shards(
    tiles, tile_slide, tile_mask, tile_label, attack_field, lift_weight, group_weight, class_weight
):
    devices = lax.axis_size("tiles")
    field = attack_field.reshape(-1, 128)
    slides = attack_field.shape[0] // PIX
    message = pl.pallas_call(
        functools.partial(pack_kernel, slides),
        out_shape=jax.ShapeDtypeStruct((devices, ROWS, 128), BF16),
        in_specs=[pl.BlockSpec(memory_space=pltpu.SMEM)] * 3 + vmem(2),
        out_specs=pl.BlockSpec(memory_space=pltpu.VMEM),
        name="pack",
    )(tile_slide, tile_mask, tile_label, tiles, field)
    got = lax.all_to_all(message, "tiles", split_axis=0, concat_axis=0, tiled=True)
    hbm = pl.BlockSpec(memory_space=pltpu.HBM)
    ahead, turned, forward, backward, fields, classes, mean = pl.pallas_call(
        weight_kernel,
        out_shape=(
            jax.ShapeDtypeStruct((9, 8, 128, 128), BF16),
            pltpu.HBM((9, 11, 128, 128), BF16),
            jax.ShapeDtypeStruct((144, 384), BF16),
            jax.ShapeDtypeStruct((80, 1152), BF16),
            jax.ShapeDtypeStruct((128, 128), BF16),
            jax.ShapeDtypeStruct((128, 128), BF16),
            jax.ShapeDtypeStruct((1, 128), F32),
        ),
        in_specs=[hbm] * 4,
        out_specs=(*vmem(1), hbm, *vmem(5)),
        scratch_shapes=[
            pltpu.VMEM((9, 8, 128, 128), BF16),
            pltpu.VMEM((9, 3, 128), F32),
            pltpu.VMEM(field.shape, F32),
            pltpu.VMEM(class_weight.shape[::-1], F32),
            pltpu.VMEM((9, 11, 128, 128), BF16),
            pltpu.SemaphoreType.DMA((9,)),
            pltpu.SemaphoreType.DMA((3,)),
            pltpu.SemaphoreType.DMA((9,)),
        ],
        compiler_params=pltpu.CompilerParams(vmem_limit_bytes=16 * 2**20),
        cost_estimate=pl.CostEstimate(flops=10_000_000, bytes_accessed=9_000_000, transcendentals=0),
        name="weights",
    )(in_hbm(group_weight), in_hbm(lift_weight), in_hbm(field), in_hbm(class_weight.T))
    spots = devices + SLOTS // 2 + GROUP // 2
    margins, attack_grad = pl.pallas_call(
        functools.partial(main_kernel, class_weight.shape[1]),
        out_shape=(jax.ShapeDtypeStruct(tile_slide.shape, F32), jax.ShapeDtypeStruct(field.shape, F32)),
        in_specs=vmem(7) + [hbm],
        out_specs=tuple(vmem(2)),
        scratch_shapes=[
            pltpu.VMEM((9, 11, 128, 128), BF16),
            pltpu.VMEM((9, 3, 128, 128), BF16),
            pltpu.VMEM((8, devices * 8), F32),
            *[pltpu.VMEM((spots, 8, 128), F32) for _ in range(5)],
            pltpu.VMEM((2, 8, 8, 384), F32),
            pltpu.VMEM((4, 128, 1024), F32),
            *[pltpu.VMEM((3, 160, 1024), BF16) for _ in range(3)],
            *[pltpu.VMEM((128, 1024), F32) for _ in range(3)],
            pltpu.VMEM((2, 8, 8, 1152), F32),
            pltpu.VMEM((16, 128), F32),
            pltpu.VMEM((16, 128), F32),
            pltpu.VMEM((spots, 16, 128), F32),
            pltpu.SemaphoreType.DMA,
        ],
        compiler_params=pltpu.CompilerParams(vmem_limit_bytes=32 * 2**20),
        cost_estimate=pl.CostEstimate(flops=4_000_000_000, bytes_accessed=9_000_000, transcendentals=2_000_000),
        name="attack",
    )(got, ahead, forward, backward, fields, classes, mean, in_hbm(turned))
    return (margins, attack_grad.reshape(-1))


def solution(mesh):
    return jax.shard_map(
        shards,
        mesh=mesh,
        in_specs=(
            P(None, ("groups", "tiles")),
            P(("groups", "tiles")),
            P(("groups", "tiles")),
            P(("groups", "tiles")),
            P(("groups", "tiles")),
            P(),
            P(),
            P(),
        ),
        out_specs=(P(("groups", "tiles")), P(("groups", "tiles"))),
        check_vma=False,
    )
```
